32 devices in a mesh: space: 4 (over y, x), tm: 8 (over z, core).
Axes of the slice: x: 2, y: 2, z: 4, core: 2. Of those that a mesh axis runs over, the one named last changes fastest.
Arguments:
- forcing: float32 [16, 96, 20, 128], P('tm', 'space'), may hold values from -6 to 6
- observed: float32 [16, 96, 20, 128], P('tm', 'space'), may hold values from -6 to 6
- jacobian: bfloat16 [16, 96, 7, 128, 128], P('tm', 'space'), may hold values from -0.078125 to 0.078125
- block_index: int32 [96, 7], P('space'), may hold values from 0 to 27, as said below
- send_list: int32 [16, 1], P('space'), may hold values from 0 to 23
- damping: float32 [96, 128], P('space'), may hold values from 0.5 to 0.9
- error_weight: float32 [96, 128], P('space'), may hold values from 0.5 to 2
- forcing_weight: float32 [128], replicated, may hold values from 0.5 to 2
Outputs:
- trajectory: float32 [16, 96, 20, 128], P('tm', 'space')
- gradient: float32 [16, 96, 20, 128], P('tm', 'space')
The draws below stay inside these ranges and needn't reach their ends.
Inputs may be any that keep to these rules, and one draw needn't show every extreme that they name: `block_index`: block 0 of every column reads the column itself; each received column is read by exactly one block of its partition.
All inputs are finite; a program needn't handle non-finite values.
Results may differ from the reference program's by a relative error of at most 0.0045.
Values may be sent and summed in bfloat16 or wider, within the bound.
A program may use at most 64 MiB of HBM per device.

```python
import math
import jax
import jax.numpy as jnp
from jax import lax

LEV = 128
NEIGH = 7
HOPS = 4
COLS_DEV = 24
MEMBERS = 20
BORDER = 1
COLS = 96
STEPS = 16
N_SPACE = 4


def draw_block_index(key, part):
    local = jax.random.randint(key, (COLS, NEIGH), 0, COLS_DEV, dtype=jnp.int32)
    column = (jnp.arange(COLS, dtype=jnp.int32) % COLS_DEV)[:, None]
    blocks = jnp.arange(NEIGH, dtype=jnp.int32)[None, :]
    slot = column + COLS_DEV * (NEIGH - 1 - blocks)
    received = HOPS * BORDER
    chosen = jnp.where(blocks == 0, column, local)
    return jnp.where(slot < received, COLS_DEV + slot, chosen).astype(jnp.int32)


def set_ends(values, key, least, largest):
    spot = [jax.random.randint(jax.random.fold_in(key, axis), (), 0, length) for axis, length in enumerate(values.shape)]
    widest = values.shape.index(max(values.shape))
    next_to = spot[:widest] + [(spot[widest] + 1) % values.shape[widest]] + spot[widest + 1:]
    return values.at[tuple(spot)].set(least).at[tuple(next_to)].set(largest)


def levels(own_key, dims, shards, low, high):
    level = 1.0
    for dim, parts in shards:
        heights = jax.random.uniform(jax.random.fold_in(jax.random.fold_in(own_key, 6), dim), (parts,), jnp.float32, low / len(shards), high / len(shards))
        level = level * jnp.repeat(jnp.exp(heights), dims[dim] // parts).reshape((-1,) + (1,) * (len(dims) - 1 - dim))
    return level


def scatter_about(own_key, dims, width, bound, shards=(), held_as=jnp.bfloat16):
    values = width * jax.random.normal(own_key, dims, jnp.float32)
    if shards:
        values = values * levels(own_key, dims, shards, -0.22, 0.18)
    return jnp.clip(values, -bound, bound).astype(held_as)


def setup_inputs(seed: int = 0) -> dict:
    arg_keys = jax.random.split(jax.random.key(seed), 9)
    forcing = scatter_about(arg_keys[0], (STEPS, COLS, MEMBERS, LEV), 1.0, 6.0, ((0, 8), (1, 4)), jnp.float32)
    observed = scatter_about(arg_keys[1], (STEPS, COLS, MEMBERS, LEV), 1.0, 6.0, ((0, 8), (1, 4)), jnp.float32)
    jacobian = scatter_about(arg_keys[2], (STEPS, COLS, NEIGH, LEV, LEV), (6 * LEV * NEIGH) ** -0.5, 0.078125, ((0, 8), (1, 4)))
    block_index = draw_block_index(jax.random.fold_in(arg_keys[8], 71), 0)
    send_list = set_ends(jax.random.randint(arg_keys[4], (N_SPACE * HOPS, BORDER), 0, COLS_DEV), jax.random.fold_in(arg_keys[4], 1), 0, COLS_DEV - 1).astype(jnp.int32)
    damping = jnp.clip(0.5 + 0.39999998 * jax.random.uniform(arg_keys[5], (COLS, LEV), jnp.float32) ** levels(arg_keys[5], (COLS, LEV), ((0, 4),), -0.2, 0.2), 0.5, 0.9)
    error_weight = jnp.clip(jnp.exp(math.log(2.0) - 1.3862944 * jax.random.uniform(arg_keys[6], (COLS, LEV), jnp.float32) ** levels(arg_keys[6], (COLS, LEV), ((0, 4),), -0.2, 0.2)), 0.5, 2.0)
    forcing_weight = jnp.clip(jnp.exp(jax.random.uniform(arg_keys[7], (LEV,), jnp.float32, math.log(0.5), math.log(2.0))), 0.5, 2.0)
    return {"forcing": forcing, "observed": observed, "jacobian": jacobian, "block_index": block_index, "send_list": send_list, "damping": damping, "error_weight": error_weight, "forcing_weight": forcing_weight}


def sources(block_index, send_list):
    offsets = jnp.array([1, -1, 2, -2], dtype=jnp.int32)
    part = (jnp.arange(COLS, dtype=jnp.int32) // COLS_DEV)[:, None]
    local = block_index < COLS_DEV
    remote = jnp.maximum(block_index - COLS_DEV, 0)
    hop_id = remote // BORDER
    within = remote % BORDER
    anchor = jnp.mod(part - offsets[hop_id], N_SPACE).astype(jnp.int32)
    remote_col = send_list[anchor * HOPS + hop_id, within]
    return jnp.where(local, part * COLS_DEV + block_index, anchor * COLS_DEV + remote_col).astype(jnp.int32)


def reference(forcing, observed, jacobian, block_index, send_list, damping, error_weight, forcing_weight):
    source = sources(block_index, send_list)

    def forward(current, inputs):
        blocks, push = inputs
        rounded = current.astype(jnp.bfloat16).astype(jnp.float32)
        picked = rounded[source]
        mixed = jnp.einsum("ckmj,ckij->cmi", picked, blocks.astype(jnp.float32))
        result = damping[:, None, :] * current + mixed + push
        return result, result

    start = jnp.zeros(forcing.shape[1:], jnp.float32)
    last_state, trajectory = lax.scan(forward, start, (jacobian, forcing))
    misfit = error_weight[None, :, None, :] * (trajectory - observed)

    def backward(carried, inputs):
        blocks, miss = inputs
        adjoint = miss + carried
        rounded = adjoint.astype(jnp.bfloat16).astype(jnp.float32)
        spread = jnp.einsum("cmi,ckij->ckmj", rounded, blocks.astype(jnp.float32))
        summed = jax.ops.segment_sum(spread.reshape((-1,) + adjoint.shape[1:]), source.reshape(-1), num_segments=COLS)
        return damping[:, None, :] * adjoint + summed, adjoint

    last_term, adjoints = lax.scan(backward, start, (jacobian, misfit), reverse=True)
    gradient = forcing_weight * forcing + adjoints
    return trajectory, gradient
```

```python
import functools
import jax
import jax.numpy as jnp
from jax import lax
from jax.experimental import pallas as pl
from jax.experimental.pallas import tpu as pltpu
from jax.sharding import PartitionSpec as P

OFFSETS = (1, -1, 2, -2)
ROWS = 32
MESH = pl.DeviceIdType.MESH
F32 = jnp.float32
BF16 = jnp.bfloat16


class Tables:
    def __init__(self, cols, neigh, hops):
        blocks = cols * neigh
        self.source = 0
        self.perm = self.source + blocks
        self.column = self.perm + blocks
        self.keep = self.column + blocks
        self.last = self.keep + blocks
        self.reads = self.last + cols
        self.listed = self.reads + cols * hops
        self.send = self.listed + cols * hops


def index_tables(block_index, send_list):
    cols, neigh = block_index.shape
    hops = send_list.shape[0]
    blocks = cols * neigh
    flat = block_index.reshape(-1)
    number = jnp.arange(blocks, dtype=jnp.int32)
    key = flat * blocks + number
    rank = jnp.sum((key[None, :] < key[:, None]).astype(jnp.int32), axis=1)
    chosen = rank[None, :] == number[:, None]
    perm = jnp.sum(jnp.where(chosen, number[None, :], 0), axis=1)
    ordered = jnp.sum(jnp.where(chosen, flat[None, :], 0), axis=1)
    keep = jnp.concatenate([jnp.zeros((1,), jnp.int32), (ordered[1:] == ordered[:-1]).astype(jnp.int32)])
    column = jnp.arange(cols, dtype=jnp.int32)
    upto = jnp.sum((flat[None, :] <= column[:, None]).astype(jnp.int32), axis=1)
    own = jnp.sum((flat[None, :] == column[:, None]).astype(jnp.int32), axis=1)
    last = jnp.where(own > 0, upto - 1, blocks)
    source = jnp.where(flat < cols, flat, cols)
    hop = jnp.arange(hops, dtype=jnp.int32)
    reads = jnp.any(block_index[:, :, None] == (cols + hop)[None, None, :], axis=1).astype(jnp.int32)
    listed = (send_list[:, 0][None, :] == column[:, None]).astype(jnp.int32)
    parts = [source, perm, perm // neigh, keep, last, reads.reshape(-1), listed.reshape(-1), send_list.reshape(-1)]
    return jnp.concatenate(parts)


def kernel(
    sizes,
    tab, forcing, observed, jac_hbm, damping, error_weight, forcing_weight,
    traj, grad,
    jac, xin, xb, halo, halo_out, adj, adj_b, sums, back, back_out, cin, cout,
    jac_sem, halo_send, halo_recv, hand_send, hand_recv,
    back_send, back_recv, cin_send, cin_recv,
):
    space, count = sizes
    steps, cols, members, lev = forcing.shape
    neigh = jac[0].shape[0] // cols
    hops = halo.shape[1]
    blocks = cols * neigh
    at = Tables(cols, neigh, hops)
    me = lax.axis_index("space")
    turn = lax.axis_index("tm")
    is_first = turn == 0
    is_last = turn == count - 1
    group = max(g for g in range(1, min(cols, 6) + 1) if cols % g == 0)
    per = group * neigh

    def place(distance, later):
        return {"space": lax.rem(me + distance + 2 * space, space), "tm": turn + later}

    def jac_copy(s):
        return pltpu.make_async_copy(jac_hbm.at[s], jac[s], jac_sem.at[s])

    def halo_copy(s, hop, later, landing):
        return pltpu.make_async_remote_copy(
            src_ref=halo_out.at[s, hop], dst_ref=halo.at[landing, hop],
            send_sem=halo_send.at[s, hop], recv_sem=halo_recv.at[landing, hop],
            device_id=place(OFFSETS[hop], later), device_id_type=MESH)

    def hand_copy():
        return pltpu.make_async_remote_copy(
            src_ref=traj.at[steps - 1], dst_ref=xin, send_sem=hand_send, recv_sem=hand_recv,
            device_id=place(0, 1), device_id_type=MESH)

    def back_copy(s, hop, later, landing):
        return pltpu.make_async_remote_copy(
            src_ref=back_out.at[s, hop], dst_ref=back.at[landing, hop],
            send_sem=back_send.at[s, hop], recv_sem=back_recv.at[landing, hop],
            device_id=place(-OFFSETS[hop], later), device_id_type=MESH)

    def cin_copy():
        return pltpu.make_async_remote_copy(
            src_ref=cout, dst_ref=cin, send_sem=cin_send, recv_sem=cin_recv,
            device_id=place(0, -1), device_id_type=MESH)

    @pl.when(jnp.logical_not(is_first))
    def _():
        jac_copy(0).start()

    for s in range(1, steps):
        jac_copy(s).start()

    barrier = pltpu.get_barrier_semaphore()

    def greet(later):
        for distance in OFFSETS + ((0,) if later else ()):
            pl.semaphore_signal(barrier, inc=1, device_id=place(distance, later), device_id_type=MESH)

    greet(0)

    @pl.when(jnp.logical_not(is_first))
    def _():
        greet(-1)

    @pl.when(jnp.logical_not(is_last))
    def _():
        greet(1)

    for s in range(steps):
        xb[s, cols] = jnp.zeros((ROWS, lev), BF16)
    sums[blocks] = jnp.zeros((members, lev), F32)
    sides = jnp.where(is_first, 0, 1) + jnp.where(is_last, 0, 1)
    pl.semaphore_wait(barrier, hops + sides * (hops + 1))

    def scalar(index):
        return tab[index].astype(F32)

    def advance(s, before):
        def some(g, carry):
            for i in range(group):
                c = g * group + i
                picked = [xb[s, tab[at.source + c * neigh + k]] for k in range(neigh)]
                held = [jac[s][c * neigh + k] for k in range(neigh)]
                mixed = lax.dot_general(
                    jnp.concatenate(picked, axis=1), jnp.concatenate(held, axis=1),
                    (((1,), (1,)), ((), ())), preferred_element_type=F32)
                damp = damping[pl.ds(c, 1), :]
                traj[s, c] = damp * before[c] + forcing[s, c] + mixed[:members]
            return carry

        lax.fori_loop(0, cols // group, some, 0)
        remote = []
        for hop in range(hops):
            halo_copy(0, hop, 0, s).wait_recv()
        for hop in range(hops):
            block = tab[at.perm + blocks - hops + hop]
            remote.append(lax.dot_general(
                halo[s, hop], jac[s][block], (((1,), (1,)), ((), ())),
                preferred_element_type=F32)[:members])
        for c in range(cols):
            value = traj[s, c]
            for hop in range(hops):
                value = value + scalar(at.reads + c * hops + hop) * remote[hop]
            traj[s, c] = value

    def hand_on(s):
        for hop in range(hops):
            halo_out[s, hop, 0:members] = traj[s, tab[at.send + hop]].astype(BF16)
        if s < steps - 1:
            for hop in range(hops):
                halo_copy(s, hop, 0, s + 1).start()
            for c in range(cols):
                xb[s + 1, c, 0:members] = traj[s, c].astype(BF16)
        else:
            @pl.when(jnp.logical_not(is_last))
            def _():
                for hop in range(hops):
                    halo_copy(s, hop, 1, 0).start()
                hand_copy().start()

    @pl.when(is_first)
    def _():
        for c in range(cols):
            traj[0, c] = forcing[0, c]

    @pl.when(jnp.logical_not(is_first))
    def _():
        jac_copy(0).wait()
        hand_copy().wait_recv()
        for c in range(cols):
            xb[0, c, 0:members] = xin[c].astype(BF16)
        advance(0, xin)

    hand_on(0)
    for s in range(1, steps):
        jac_copy(s).wait()
        advance(s, traj.at[s - 1])
        hand_on(s)

    def misfit(s, c):
        return error_weight[pl.ds(c, 1), :] * (traj[s, c] - observed[s, c])

    def with_back(landing, c, value):
        for hop in range(hops):
            value = value + scalar(at.listed + c * hops + hop) * back[landing, hop]
        return value

    def keep_adjoint(s, c, value):
        adj[c] = value
        adj_b[c, 0:members] = value.astype(BF16)
        grad[s, c] = forcing_weight[...] * forcing[s, c] + value

    def transpose_step(s):
        for hop in range(hops):
            spot = blocks - hops + hop
            back_out[s, hop] = jnp.dot(
                adj_b[tab[at.column + spot]], jac[s][tab[at.perm + spot]],
                preferred_element_type=F32)[:members]
            if s > 0:
                back_copy(s, hop, 0, s - 1).start()
            else:
                back_copy(s, hop, -1, steps - 1).start()

        def some(g, total):
            for i in range(per):
                b = g * per + i
                spread = jnp.dot(
                    adj_b[tab[at.column + b]], jac[s][tab[at.perm + b]],
                    preferred_element_type=F32)[:members]
                total = spread + scalar(at.keep + b) * total
                sums[b] = total
            return total

        lax.fori_loop(0, cols // group, some, jnp.zeros((members, lev), F32))
        for c in range(cols):
            cout[c] = damping[pl.ds(c, 1), :] * adj[c] + sums[tab[at.last + c]]

    @pl.when(is_last)
    def _():
        for c in range(cols):
            keep_adjoint(steps - 1, c, misfit(steps - 1, c))

    @pl.when(jnp.logical_not(is_last))
    def _():
        for hop in range(hops):
            back_copy(0, hop, 0, steps - 1).wait_recv()
        cin_copy().wait_recv()
        for c in range(cols):
            keep_adjoint(steps - 1, c, with_back(steps - 1, c, misfit(steps - 1, c) + cin[c]))

    for s in range(steps - 1, 0, -1):
        transpose_step(s)
        for hop in range(hops):
            back_copy(0, hop, 0, s - 1).wait_recv()
        for c in range(cols):
            keep_adjoint(s - 1, c, with_back(s - 1, c, misfit(s - 1, c) + cout[c]))

    @pl.when(jnp.logical_not(is_first))
    def _():
        transpose_step(0)
        cin_copy().start()
        for hop in range(hops):
            back_copy(0, hop, -1, steps - 1).wait_send()
        cin_copy().wait_send()

    for s in range(1, steps):
        for hop in range(hops):
            back_copy(s, hop, 0, s - 1).wait_send()
            halo_copy(s - 1, hop, 0, s).wait_send()

    @pl.when(jnp.logical_not(is_last))
    def _():
        for hop in range(hops):
            halo_copy(steps - 1, hop, 1, 0).wait_send()
        hand_copy().wait_send()


def on_device(
    sizes, forcing, observed, jacobian, block_index, send_list, damping, error_weight, forcing_weight
):
    steps, cols, members, lev = forcing.shape
    neigh = jacobian.shape[2]
    hops = send_list.shape[0]
    blocks = cols * neigh
    tab = index_tables(block_index, send_list)
    vmem = pl.BlockSpec(memory_space=pltpu.VMEM)
    state = (cols, members, lev)
    dma = pltpu.SemaphoreType.DMA
    return pl.pallas_call(
        functools.partial(kernel, sizes),
        out_shape=(jax.ShapeDtypeStruct(forcing.shape, F32),) * 2,
        in_specs=[
            pl.BlockSpec(memory_space=pltpu.SMEM), vmem, vmem,
            pl.BlockSpec(memory_space=pl.ANY), vmem, vmem, vmem,
        ],
        out_specs=(vmem, vmem),
        scratch_shapes=[
            [pltpu.VMEM((blocks, lev, lev), BF16) for _ in range(steps)],
            pltpu.VMEM(state, F32),
            pltpu.VMEM((steps, cols + 1, ROWS, lev), BF16),
            pltpu.VMEM((steps, hops, ROWS, lev), BF16),
            pltpu.VMEM((steps, hops, ROWS, lev), BF16),
            pltpu.VMEM(state, F32),
            pltpu.VMEM((cols, ROWS, lev), BF16),
            pltpu.VMEM((blocks + 1, members, lev), F32),
            pltpu.VMEM((steps, hops, members, lev), F32),
            pltpu.VMEM((steps, hops, members, lev), F32),
            pltpu.VMEM(state, F32),
            pltpu.VMEM(state, F32),
            dma((steps,)),
            dma((steps, hops)), dma((steps, hops)), dma(()), dma(()),
            dma((steps, hops)), dma((steps, hops)), dma(()), dma(()),
        ],
        compiler_params=pltpu.CompilerParams(
            collective_id=0, has_side_effects=True, vmem_limit_bytes=48 * 1024 * 1024),
    )(
        tab, forcing, observed, jacobian.reshape(steps, blocks, lev, lev),
        damping, error_weight, forcing_weight.reshape(1, lev),
    )


def solution(mesh):
    sizes = (mesh.shape["space"], mesh.shape["tm"])
    in_specs = (
        P("tm", "space", None, None),
        P("tm", "space", None, None),
        P("tm", "space", None, None, None),
        P("space", None),
        P("space", None),
        P("space", None),
        P("space", None),
        P(),
    )
    out_specs = (P("tm", "space", None, None), P("tm", "space", None, None))
    return jax.shard_map(
        functools.partial(on_device, sizes), mesh=mesh, in_specs=in_specs, out_specs=out_specs,
        check_vma=False,
    )
```

```python
import functools
import jax
import jax.numpy as jnp
from jax import lax
from jax.experimental import pallas as pl
from jax.experimental.pallas import tpu as pltpu
from jax.sharding import PartitionSpec as P

OFFSETS = (1, -1, 2, -2)
ROWS = 32
MESH = pl.DeviceIdType.MESH
F32 = jnp.float32
BF16 = jnp.bfloat16


class Tables:
    def __init__(self, cols, neigh, hops):
        blocks = cols * neigh
        self.source = 0
        self.perm = self.source + blocks
        self.column = self.perm + blocks
        self.keep = self.column + blocks
        self.last = self.keep + blocks
        self.reads = self.last + cols
        self.listed = self.reads + cols
        self.send = self.listed + cols


def index_tables(block_index, send_list):
    cols, neigh = block_index.shape
    hops = send_list.shape[0]
    blocks = cols * neigh
    flat = block_index.reshape(-1)
    number = jnp.arange(blocks, dtype=jnp.int32)
    key = flat * blocks + number
    rank = jnp.sum((key[None, :] < key[:, None]).astype(jnp.int32), axis=1)
    chosen = rank[None, :] == number[:, None]
    perm = jnp.sum(jnp.where(chosen, number[None, :], 0), axis=1)
    ordered = jnp.sum(jnp.where(chosen, flat[None, :], 0), axis=1)
    keep = jnp.concatenate([jnp.zeros((1,), jnp.int32), (ordered[1:] == ordered[:-1]).astype(jnp.int32)])
    column = jnp.arange(cols, dtype=jnp.int32)
    upto = jnp.sum((flat[None, :] <= column[:, None]).astype(jnp.int32), axis=1)
    own = jnp.sum((flat[None, :] == column[:, None]).astype(jnp.int32), axis=1)
    last = jnp.where(own > 0, upto - 1, blocks)
    source = jnp.where(flat < cols, flat, cols)
    hop = jnp.arange(hops, dtype=jnp.int32)
    reads = jnp.any(block_index[:, :, None] == (cols + hop)[None, None, :], axis=1)
    reads = jnp.sum(jnp.where(reads, 1 << hop, 0), axis=1)
    listed = jnp.sum(jnp.where(send_list[:, 0][None, :] == column[:, None], 1 << hop, 0), axis=1)
    parts = [source, perm, perm // neigh, keep, last, reads, listed, send_list.reshape(-1)]
    return jnp.concatenate(parts)


def kernel(
    sizes,
    tab, forcing, observed, jac_hbm, damping, error_weight, forcing_weight,
    traj, grad,
    misfit, subset, jac, xin, xb, halo, halo_out, adj, adj_b, sums, back, back_out, cin, cout,
    jac_sem, halo_send, halo_recv, hand_send, hand_recv,
    back_send, back_recv, cin_send, cin_recv,
):
    space, count = sizes
    steps, cols, members, lev = forcing.shape
    neigh = jac[0].shape[0] // cols
    hops = halo.shape[1]
    blocks = cols * neigh
    at = Tables(cols, neigh, hops)
    me = lax.axis_index("space")
    turn = lax.axis_index("tm")
    is_first = turn == 0
    is_last = turn == count - 1
    pair = 2 if cols % 2 == 0 else 1
    pairs = cols // pair
    group = pairs // 2 if pairs % 2 == 0 else pairs
    tiles = 4 if blocks % 4 == 0 else 1
    half = blocks // tiles // 2 if blocks // tiles % 2 == 0 else blocks // tiles

    def place(distance, later):
        return {"space": lax.rem(me + distance + 2 * space, space), "tm": turn + later}

    def jac_copy(s):
        return pltpu.make_async_copy(jac_hbm.at[s], jac[s], jac_sem.at[s])

    def halo_copy(s, hop, later, landing):
        return pltpu.make_async_remote_copy(
            src_ref=halo_out.at[s, hop], dst_ref=halo.at[landing, hop],
            send_sem=halo_send.at[s, hop], recv_sem=halo_recv.at[landing, hop],
            device_id=place(OFFSETS[hop], later), device_id_type=MESH)

    def hand_copy():
        return pltpu.make_async_remote_copy(
            src_ref=traj.at[steps - 1], dst_ref=xin, send_sem=hand_send, recv_sem=hand_recv,
            device_id=place(0, 1), device_id_type=MESH)

    def back_copy(s, hop, later, landing):
        return pltpu.make_async_remote_copy(
            src_ref=back_out.at[s, hop], dst_ref=back.at[landing, hop],
            send_sem=back_send.at[s, hop], recv_sem=back_recv.at[landing, hop],
            device_id=place(-OFFSETS[hop], later), device_id_type=MESH)

    def cin_copy():
        return pltpu.make_async_remote_copy(
            src_ref=cout, dst_ref=cin, send_sem=cin_send, recv_sem=cin_recv,
            device_id=place(0, -1), device_id_type=MESH)

    @pl.when(jnp.logical_not(is_first))
    def _():
        jac_copy(0).start()

    for s in range(1, steps):
        jac_copy(s).start()

    barrier = pltpu.get_barrier_semaphore()

    def greet(later):
        for distance in OFFSETS + ((0,) if later else ()):
            pl.semaphore_signal(barrier, inc=1, device_id=place(distance, later), device_id_type=MESH)

    greet(0)

    @pl.when(jnp.logical_not(is_first))
    def _():
        greet(-1)

    @pl.when(jnp.logical_not(is_last))
    def _():
        greet(1)

    for s in range(steps):
        xb[s, cols] = jnp.zeros((ROWS, lev), BF16)
    sums[blocks] = jnp.zeros((members, lev), F32)
    sides = jnp.where(is_first, 0, 1) + jnp.where(is_last, 0, 1)
    pl.semaphore_wait(barrier, hops + sides * (hops + 1))

    def scalar(index):
        return tab[index].astype(F32)

    def subset_sums(terms):
        held = [jnp.zeros((members, lev), F32)]
        for term in terms:
            held = held + [term if i == 0 else value + term for i, value in enumerate(held)]
        for i, value in enumerate(held):
            subset[i] = value

    def advance(s, before):
        def some(g, carry):
            for i in range(group):
                first = (g * group + i) * pair
                left, right = [], []
                for c in range(pair):
                    here = (first + c) * neigh
                    left.append(jnp.concatenate([xb[s, tab[at.source + here + k]] for k in range(neigh)], axis=1))
                    right.append(jnp.concatenate([jac[s][here + k] for k in range(neigh)], axis=1))
                mixed = lax.dot_general(
                    jnp.concatenate(left, axis=0), jnp.concatenate(right, axis=0),
                    (((1,), (1,)), ((), ())), preferred_element_type=F32)
                for c in range(pair):
                    column = first + c
                    damp = damping[pl.ds(column, 1), :]
                    own = mixed[c * ROWS : c * ROWS + members, c * lev : (c + 1) * lev]
                    traj[s, column] = damp * before[column] + forcing[s, column] + own
            return carry

        lax.fori_loop(0, pairs // group, some, 0)
        remote = []
        for hop in range(hops):
            halo_copy(0, hop, 0, s).wait_recv()
        for hop in range(hops):
            block = tab[at.perm + blocks - hops + hop]
            remote.append(lax.dot_general(
                halo[s, hop], jac[s][block], (((1,), (1,)), ((), ())),
                preferred_element_type=F32)[:members])
        subset_sums(remote)
        for c in range(cols):
            value = traj[s, c] + subset[tab[at.reads + c]]
            traj[s, c] = value
            if s < steps - 1:
                xb[s + 1, c, 0:members] = value.astype(BF16)

    def hand_on(s):
        for hop in range(hops):
            halo_out[s, hop, 0:members] = traj[s, tab[at.send + hop]].astype(BF16)
        if s < steps - 1:
            for hop in range(hops):
                halo_copy(s, hop, 0, s + 1).start()
        else:
            @pl.when(jnp.logical_not(is_last))
            def _():
                for hop in range(hops):
                    halo_copy(s, hop, 1, 0).start()
                hand_copy().start()

    @pl.when(is_first)
    def _():
        for c in range(cols):
            traj[0, c] = forcing[0, c]
            if steps > 1:
                xb[1, c, 0:members] = forcing[0, c].astype(BF16)

    @pl.when(jnp.logical_not(is_first))
    def _():
        jac_copy(0).wait()
        hand_copy().wait_recv()
        for c in range(cols):
            xb[0, c, 0:members] = xin[c].astype(BF16)
        advance(0, xin)

    hand_on(0)
    for s in range(1, steps):
        jac_copy(s).wait()
        advance(s, traj.at[s - 1])
        hand_on(s)

    for s in range(steps):
        for c in range(cols):
            misfit[s, c] = error_weight[pl.ds(c, 1), :] * (traj[s, c] - observed[s, c])

    def add_back(landing):
        subset_sums([back[landing, hop] for hop in range(hops)])

    def keep_adjoint(s, c, value):
        adj[c] = value
        adj_b[c, 0:members] = value.astype(BF16)
        grad[s, c] = forcing_weight[...] * forcing[s, c] + value

    def transpose_step(s):
        for hop in range(hops):
            spot = blocks - hops + hop
            back_out[s, hop] = jnp.dot(
                adj_b[tab[at.column + spot]], jac[s][tab[at.perm + spot]],
                preferred_element_type=F32)[:members]
            if s > 0:
                back_copy(s, hop, 0, s - 1).start()
            else:
                back_copy(s, hop, -1, steps - 1).start()

        blank = jnp.zeros((ROWS, lev), BF16)

        def some(g, total):
            for i in range(half):
                first = (g * half + i) * tiles
                turned = [adj_b[tab[at.column + first + n]] for n in range(tiles)]
                held = [jac[s][tab[at.perm + first + n]] for n in range(tiles)]
                if tiles == 4:
                    left = [jnp.concatenate([w, blank], axis=1) for w in turned[:2]]
                    left += [jnp.concatenate([blank, w], axis=1) for w in turned[2:]]
                    left = jnp.concatenate(left, axis=0)
                    upper = jnp.concatenate(held[:2], axis=1)
                    lower = jnp.concatenate(held[2:], axis=1)
                    right = jnp.concatenate([upper, lower], axis=0)
                else:
                    left, right = turned[0], held[0]
                spread = jnp.dot(left, right, preferred_element_type=F32)
                for n in range(tiles):
                    lane = n % 2 * lev
                    part = spread[n * ROWS : n * ROWS + members, lane : lane + lev]
                    total = part + scalar(at.keep + first + n) * total
                    sums[first + n] = total
            return total

        lax.fori_loop(0, blocks // tiles // half, some, jnp.zeros((members, lev), F32))
        for c in range(cols):
            cout[c] = damping[pl.ds(c, 1), :] * adj[c] + sums[tab[at.last + c]]

    @pl.when(is_last)
    def _():
        for c in range(cols):
            keep_adjoint(steps - 1, c, misfit[steps - 1, c])

    @pl.when(jnp.logical_not(is_last))
    def _():
        for hop in range(hops):
            back_copy(0, hop, 0, steps - 1).wait_recv()
        add_back(steps - 1)
        cin_copy().wait_recv()
        for c in range(cols):
            value = misfit[steps - 1, c] + cin[c] + subset[tab[at.listed + c]]
            keep_adjoint(steps - 1, c, value)

    for s in range(steps - 1, 0, -1):
        transpose_step(s)
        for hop in range(hops):
            back_copy(0, hop, 0, s - 1).wait_recv()
        add_back(s - 1)
        for c in range(cols):
            keep_adjoint(s - 1, c, misfit[s - 1, c] + cout[c] + subset[tab[at.listed + c]])

    @pl.when(jnp.logical_not(is_first))
    def _():
        transpose_step(0)
        cin_copy().start()
        for hop in range(hops):
            back_copy(0, hop, -1, steps - 1).wait_send()
        cin_copy().wait_send()

    for s in range(1, steps):
        for hop in range(hops):
            back_copy(s, hop, 0, s - 1).wait_send()
            halo_copy(s - 1, hop, 0, s).wait_send()

    @pl.when(jnp.logical_not(is_last))
    def _():
        for hop in range(hops):
            halo_copy(steps - 1, hop, 1, 0).wait_send()
        hand_copy().wait_send()


def on_device(
    sizes, forcing, observed, jacobian, block_index, send_list, damping, error_weight, forcing_weight
):
    steps, cols, members, lev = forcing.shape
    neigh = jacobian.shape[2]
    hops = send_list.shape[0]
    blocks = cols * neigh
    tab = index_tables(block_index, send_list)
    vmem = pl.BlockSpec(memory_space=pltpu.VMEM)
    state = (cols, members, lev)
    dma = pltpu.SemaphoreType.DMA
    return pl.pallas_call(
        functools.partial(kernel, sizes),
        out_shape=(jax.ShapeDtypeStruct(forcing.shape, F32),) * 2,
        in_specs=[
            pl.BlockSpec(memory_space=pltpu.SMEM), vmem, vmem,
            pl.BlockSpec(memory_space=pl.ANY), vmem, vmem, vmem,
        ],
        out_specs=(vmem, vmem),
        scratch_shapes=[
            pltpu.VMEM(forcing.shape, F32),
            pltpu.VMEM((2 ** hops, members, lev), F32),
            [pltpu.VMEM((blocks, lev, lev), BF16) for _ in range(steps)],
            pltpu.VMEM(state, F32),
            pltpu.VMEM((steps, cols + 1, ROWS, lev), BF16),
            pltpu.VMEM((steps, hops, ROWS, lev), BF16),
            pltpu.VMEM((steps, hops, ROWS, lev), BF16),
            pltpu.VMEM(state, F32),
            pltpu.VMEM((cols, ROWS, lev), BF16),
            pltpu.VMEM((blocks + 1, members, lev), F32),
            pltpu.VMEM((steps, hops, members, lev), F32),
            pltpu.VMEM((steps, hops, members, lev), F32),
            pltpu.VMEM(state, F32),
            pltpu.VMEM(state, F32),
            dma((steps,)),
            dma((steps, hops)), dma((steps, hops)), dma(()), dma(()),
            dma((steps, hops)), dma((steps, hops)), dma(()), dma(()),
        ],
        compiler_params=pltpu.CompilerParams(
            collective_id=0, has_side_effects=True, vmem_limit_bytes=48 * 1024 * 1024),
    )(
        tab, forcing, observed, jacobian.reshape(steps, blocks, lev, lev),
        damping, error_weight, forcing_weight.reshape(1, lev),
    )


def solution(mesh):
    sizes = (mesh.shape["space"], mesh.shape["tm"])
    in_specs = (
        P("tm", "space", None, None),
        P("tm", "space", None, None),
        P("tm", "space", None, None, None),
        P("space", None),
        P("space", None),
        P("space", None),
        P("space", None),
        P(),
    )
    out_specs = (P("tm", "space", None, None), P("tm", "space", None, None))
    return jax.shard_map(
        functools.partial(on_device, sizes), mesh=mesh, in_specs=in_specs, out_specs=out_specs,
        check_vma=False,
    )
```

```python
import functools
import jax
import jax.numpy as jnp
from jax import lax
from jax.experimental import pallas as pl
from jax.experimental.pallas import tpu as pltpu
from jax.sharding import PartitionSpec as P

OFFSETS = (1, -1, 2, -2)
ROWS = 32
MESH = pl.DeviceIdType.MESH
F32 = jnp.float32
BF16 = jnp.bfloat16


class Tables:
    def __init__(self, cols, neigh, hops):
        blocks = cols * neigh
        self.source = 0
        self.perm = self.source + blocks
        self.column = self.perm + blocks
        self.keep = self.column + blocks
        self.last = self.keep + blocks
        self.reads = self.last + cols
        self.listed = self.reads + cols
        self.send = self.listed + cols


def index_tables(block_index, send_list):
    cols, neigh = block_index.shape
    hops = send_list.shape[0]
    blocks = cols * neigh
    flat = block_index.reshape(-1)
    number = jnp.arange(blocks, dtype=jnp.int32)
    key = flat * blocks + number
    rank = jnp.sum((key[None, :] < key[:, None]).astype(jnp.int32), axis=1)
    chosen = rank[None, :] == number[:, None]
    perm = jnp.sum(jnp.where(chosen, number[None, :], 0), axis=1)
    ordered = jnp.sum(jnp.where(chosen, flat[None, :], 0), axis=1)
    keep = jnp.concatenate([jnp.zeros((1,), jnp.int32), (ordered[1:] == ordered[:-1]).astype(jnp.int32)])
    column = jnp.arange(cols, dtype=jnp.int32)
    upto = jnp.sum((flat[None, :] <= column[:, None]).astype(jnp.int32), axis=1)
    own = jnp.sum((flat[None, :] == column[:, None]).astype(jnp.int32), axis=1)
    last = jnp.where(own > 0, upto - 1, blocks)
    source = jnp.where(flat < cols, flat, cols)
    hop = jnp.arange(hops, dtype=jnp.int32)
    reads = jnp.any(block_index[:, :, None] == (cols + hop)[None, None, :], axis=1)
    reads = jnp.sum(jnp.where(reads, 1 << hop, 0), axis=1)
    listed = jnp.sum(jnp.where(send_list[:, 0][None, :] == column[:, None], 1 << hop, 0), axis=1)
    parts = [source, perm, perm // neigh, keep, last, reads, listed, send_list.reshape(-1)]
    return jnp.concatenate(parts)


def kernel(
    sizes,
    tab, forcing_hbm, observed_hbm, jac_hbm, damping_hbm, error_weight_hbm, forcing_weight_hbm,
    traj_out, grad,
    forcing, observed, damping, error_weight, forcing_weight, load_sem, traj, misfit, subset, jac, xin, xb, halo, halo_out, adj, adj_b, sums, back, back_out, cin, cout,
    jac_sem, halo_send, halo_recv, hand_send, hand_recv,
    back_send, back_recv, cin_send, cin_recv,
):
    space, count = sizes
    steps, cols, members, lev = traj.shape
    neigh = jac[0].shape[0] // cols
    hops = halo.shape[1]
    blocks = cols * neigh
    at = Tables(cols, neigh, hops)
    me = lax.axis_index("space")
    turn = lax.axis_index("tm")
    is_first = turn == 0
    is_last = turn == count - 1
    group = cols // 2 if cols % 2 == 0 else cols
    tiles = 4 if blocks % 4 == 0 else 1
    half = blocks // tiles // 2 if blocks // tiles % 2 == 0 else blocks // tiles

    def place(distance, later):
        return {"space": lax.rem(me + distance + 2 * space, space), "tm": turn + later}

    def jac_copy(s):
        return pltpu.make_async_copy(jac_hbm.at[s], jac[s], jac_sem.at[s])

    def halo_copy(s, hop, later, landing):
        return pltpu.make_async_remote_copy(
            src_ref=halo_out.at[s, hop], dst_ref=halo.at[landing, hop],
            send_sem=halo_send.at[s, hop], recv_sem=halo_recv.at[landing, hop],
            device_id=place(OFFSETS[hop], later), device_id_type=MESH)

    def hand_copy():
        return pltpu.make_async_remote_copy(
            src_ref=traj.at[steps - 1], dst_ref=xin, send_sem=hand_send, recv_sem=hand_recv,
            device_id=place(0, 1), device_id_type=MESH)

    def back_copy(s, hop, later, landing):
        return pltpu.make_async_remote_copy(
            src_ref=back_out.at[s, hop], dst_ref=back.at[landing, hop],
            send_sem=back_send.at[s, hop], recv_sem=back_recv.at[landing, hop],
            device_id=place(-OFFSETS[hop], later), device_id_type=MESH)

    def cin_copy():
        return pltpu.make_async_remote_copy(
            src_ref=cout, dst_ref=cin, send_sem=cin_send, recv_sem=cin_recv,
            device_id=place(0, -1), device_id_type=MESH)

    @pl.when(jnp.logical_not(is_first))
    def _():
        jac_copy(0).start()

    for s in range(1, steps):
        jac_copy(s).start()

    loads = [
        pltpu.make_async_copy(source, target, load_sem.at[i])
        for i, (source, target) in enumerate([
            (forcing_hbm, forcing), (damping_hbm, damping), (observed_hbm, observed),
            (error_weight_hbm, error_weight), (forcing_weight_hbm, forcing_weight)])
    ]
    for load in loads:
        load.start()

    def rows(c):
        return pl.ds(c, members, stride=cols)

    barrier = pltpu.get_barrier_semaphore()

    def greet(later):
        for distance in OFFSETS + ((0,) if later else ()):
            pl.semaphore_signal(barrier, inc=1, device_id=place(distance, later), device_id_type=MESH)

    greet(0)

    @pl.when(jnp.logical_not(is_first))
    def _():
        greet(-1)

    @pl.when(jnp.logical_not(is_last))
    def _():
        greet(1)

    for s in range(steps):
        xb[s, cols] = jnp.zeros((ROWS, lev), BF16)
    sums[blocks] = jnp.zeros((members, lev), F32)
    sides = jnp.where(is_first, 0, 1) + jnp.where(is_last, 0, 1)
    pl.semaphore_wait(barrier, hops + sides * (hops + 1))

    def scalar(index):
        return tab[index].astype(F32)

    def subset_sums(terms):
        held = [jnp.zeros((members, lev), F32)]
        for term in terms:
            held = held + [term if i == 0 else value + term for i, value in enumerate(held)]
        for i, value in enumerate(held):
            subset[i] = value

    def advance(s, before):
        def some(g, carry):
            for i in range(group):
                c = g * group + i
                picked = [xb[s, tab[at.source + c * neigh + k]] for k in range(neigh)]
                held = [jac[s][c * neigh + k] for k in range(neigh)]
                turned = lax.dot_general(
                    jnp.concatenate(held, axis=1), jnp.concatenate(picked, axis=1),
                    (((1,), (1,)), ((), ())), preferred_element_type=F32)
                mixed = jnp.transpose(turned)[:members]
                damp = damping[pl.ds(c, 1), :]
                traj[s, c] = damp * before[c] + forcing[s, rows(c), :] + mixed
            return carry

        lax.fori_loop(0, cols // group, some, 0)
        remote = []
        for hop in range(hops):
            halo_copy(0, hop, 0, s).wait_recv()
        for hop in range(hops):
            block = tab[at.perm + blocks - hops + hop]
            remote.append(lax.dot_general(
                halo[s, hop], jac[s][block], (((1,), (1,)), ((), ())),
                preferred_element_type=F32)[:members])
        subset_sums(remote)
        for c in range(cols):
            value = traj[s, c] + subset[tab[at.reads + c]]
            traj[s, c] = value
            if s < steps - 1:
                xb[s + 1, c, 0:members] = value.astype(BF16)

    def hand_on(s):
        for hop in range(hops):
            halo_out[s, hop, 0:members] = traj[s, tab[at.send + hop]].astype(BF16)
        if s < steps - 1:
            for hop in range(hops):
                halo_copy(s, hop, 0, s + 1).start()
        else:
            @pl.when(jnp.logical_not(is_last))
            def _():
                for hop in range(hops):
                    halo_copy(s, hop, 1, 0).start()
                hand_copy().start()

    for load in loads:
        load.wait()

    @pl.when(is_first)
    def _():
        for c in range(cols):
            value = forcing[0, rows(c), :]
            traj[0, c] = value
            if steps > 1:
                xb[1, c, 0:members] = value.astype(BF16)

    @pl.when(jnp.logical_not(is_first))
    def _():
        jac_copy(0).wait()
        hand_copy().wait_recv()
        for c in range(cols):
            xb[0, c, 0:members] = xin[c].astype(BF16)
        advance(0, xin)

    hand_on(0)
    for s in range(1, steps):
        jac_copy(s).wait()
        advance(s, traj.at[s - 1])
        hand_on(s)

    for s in range(steps):
        for c in range(cols):
            misfit[s, c] = error_weight[pl.ds(c, 1), :] * (traj[s, c] - observed[s, rows(c), :])
            traj_out[s, rows(c), :] = traj[s, c]

    def add_back(landing):
        subset_sums([back[landing, hop] for hop in range(hops)])

    def keep_adjoint(s, c, value):
        adj[c] = value
        adj_b[c, 0:members] = value.astype(BF16)
        grad[s, rows(c), :] = forcing_weight[...] * forcing[s, rows(c), :] + value

    def transpose_step(s):
        for hop in range(hops):
            spot = blocks - hops + hop
            back_out[s, hop] = jnp.dot(
                adj_b[tab[at.column + spot]], jac[s][tab[at.perm + spot]],
                preferred_element_type=F32)[:members]
            if s > 0:
                back_copy(s, hop, 0, s - 1).start()
            else:
                back_copy(s, hop, -1, steps - 1).start()

        blank = jnp.zeros((ROWS, lev), BF16)

        def some(g, total):
            for i in range(half):
                first = (g * half + i) * tiles
                turned = [adj_b[tab[at.column + first + n]] for n in range(tiles)]
                held = [jac[s][tab[at.perm + first + n]] for n in range(tiles)]
                if tiles == 4:
                    left = [jnp.concatenate([w, blank], axis=1) for w in turned[:2]]
                    left += [jnp.concatenate([blank, w], axis=1) for w in turned[2:]]
                    left = jnp.concatenate(left, axis=0)
                    upper = jnp.concatenate(held[:2], axis=1)
                    lower = jnp.concatenate(held[2:], axis=1)
                    right = jnp.concatenate([upper, lower], axis=0)
                else:
                    left, right = turned[0], held[0]
                spread = jnp.dot(left, right, preferred_element_type=F32)
                for n in range(tiles):
                    lane = n % 2 * lev
                    part = spread[n * ROWS : n * ROWS + members, lane : lane + lev]
                    total = part + scalar(at.keep + first + n) * total
                    sums[first + n] = total
            return total

        lax.fori_loop(0, blocks // tiles // half, some, jnp.zeros((members, lev), F32))
        for c in range(cols):
            cout[c] = damping[pl.ds(c, 1), :] * adj[c] + sums[tab[at.last + c]]

    @pl.when(is_last)
    def _():
        for c in range(cols):
            keep_adjoint(steps - 1, c, misfit[steps - 1, c])

    @pl.when(jnp.logical_not(is_last))
    def _():
        for hop in range(hops):
            back_copy(0, hop, 0, steps - 1).wait_recv()
        add_back(steps - 1)
        cin_copy().wait_recv()
        for c in range(cols):
            value = misfit[steps - 1, c] + cin[c] + subset[tab[at.listed + c]]
            keep_adjoint(steps - 1, c, value)

    for s in range(steps - 1, 0, -1):
        transpose_step(s)
        for hop in range(hops):
            back_copy(0, hop, 0, s - 1).wait_recv()
        add_back(s - 1)
        for c in range(cols):
            keep_adjoint(s - 1, c, misfit[s - 1, c] + cout[c] + subset[tab[at.listed + c]])

    @pl.when(jnp.logical_not(is_first))
    def _():
        transpose_step(0)
        cin_copy().start()
        for hop in range(hops):
            back_copy(0, hop, -1, steps - 1).wait_send()
        cin_copy().wait_send()

    for s in range(1, steps):
        for hop in range(hops):
            back_copy(s, hop, 0, s - 1).wait_send()
            halo_copy(s - 1, hop, 0, s).wait_send()

    @pl.when(jnp.logical_not(is_last))
    def _():
        for hop in range(hops):
            halo_copy(steps - 1, hop, 1, 0).wait_send()
        hand_copy().wait_send()


def on_device(
    sizes, forcing, observed, jacobian, block_index, send_list, damping, error_weight, forcing_weight
):
    steps, cols, members, lev = forcing.shape
    neigh = jacobian.shape[2]
    hops = send_list.shape[0]
    blocks = cols * neigh
    tab = index_tables(block_index, send_list)
    vmem = pl.BlockSpec(memory_space=pltpu.VMEM)
    far = pl.BlockSpec(memory_space=pl.ANY)
    flat = (steps, members * cols, lev)

    def by_member(array):
        return array.transpose(0, 2, 1, 3).reshape(flat)

    def by_column(array):
        return array.reshape(steps, members, cols, lev).transpose(0, 2, 1, 3)

    state = (cols, members, lev)
    dma = pltpu.SemaphoreType.DMA
    trajectory, gradient = pl.pallas_call(
        functools.partial(kernel, sizes),
        out_shape=(jax.ShapeDtypeStruct(flat, F32),) * 2,
        in_specs=[pl.BlockSpec(memory_space=pltpu.SMEM)] + [far] * 6,
        out_specs=(vmem, vmem),
        scratch_shapes=[
            pltpu.VMEM(flat, F32), pltpu.VMEM(flat, F32),
            pltpu.VMEM((cols, lev), F32), pltpu.VMEM((cols, lev), F32), pltpu.VMEM((1, lev), F32),
            dma((5,)),
            pltpu.VMEM(forcing.shape, F32),
            pltpu.VMEM(forcing.shape, F32),
            pltpu.VMEM((2 ** hops, members, lev), F32),
            [pltpu.VMEM((blocks, lev, lev), BF16) for _ in range(steps)],
            pltpu.VMEM(state, F32),
            pltpu.VMEM((steps, cols + 1, ROWS, lev), BF16),
            pltpu.VMEM((steps, hops, ROWS, lev), BF16),
            pltpu.VMEM((steps, hops, ROWS, lev), BF16),
            pltpu.VMEM(state, F32),
            pltpu.VMEM((cols, ROWS, lev), BF16),
            pltpu.VMEM((blocks + 1, members, lev), F32),
            pltpu.VMEM((steps, hops, members, lev), F32),
            pltpu.VMEM((steps, hops, members, lev), F32),
            pltpu.VMEM(state, F32),
            pltpu.VMEM(state, F32),
            dma((steps,)),
            dma((steps, hops)), dma((steps, hops)), dma(()), dma(()),
            dma((steps, hops)), dma((steps, hops)), dma(()), dma(()),
        ],
        compiler_params=pltpu.CompilerParams(
            collective_id=0, has_side_effects=True, vmem_limit_bytes=63 * 1024 * 1024),
    )(
        tab, by_member(forcing), by_member(observed), jacobian.reshape(steps, blocks, lev, lev),
        damping, error_weight, forcing_weight.reshape(1, lev),
    )
    return by_column(trajectory), by_column(gradient)


def solution(mesh):
    sizes = (mesh.shape["space"], mesh.shape["tm"])
    in_specs = (
        P("tm", "space", None, None),
        P("tm", "space", None, None),
        P("tm", "space", None, None, None),
        P("space", None),
        P("space", None),
        P("space", None),
        P("space", None),
        P(),
    )
    out_specs = (P("tm", "space", None, None), P("tm", "space", None, None))
    return jax.shard_map(
        functools.partial(on_device, sizes), mesh=mesh, in_specs=in_specs, out_specs=out_specs,
        check_vma=False,
    )
```

```python
import functools
import jax
import jax.numpy as jnp
from jax import lax
from jax.experimental import pallas as pl
from jax.experimental.pallas import tpu as pltpu
from jax.sharding import PartitionSpec as P

OFFSETS = (1, -1, 2, -2)
ROWS = 32
MESH = pl.DeviceIdType.MESH
F32 = jnp.float32
BF16 = jnp.bfloat16


class Tables:
    def __init__(self, cols, neigh, hops):
        blocks = cols * neigh
        self.source = 0
        self.perm = self.source + blocks
        self.column = self.perm + blocks
        self.keep = self.column + blocks
        self.last = self.keep + blocks
        self.reads = self.last + cols
        self.listed = self.reads + cols
        self.send = self.listed + cols


def index_tables(block_index, send_list):
    cols, neigh = block_index.shape
    hops = send_list.shape[0]
    blocks = cols * neigh
    flat = block_index.reshape(-1)
    number = jnp.arange(blocks, dtype=jnp.int32)
    key = flat * blocks + number
    rank = jnp.sum((key[None, :] < key[:, None]).astype(jnp.int32), axis=1)
    chosen = rank[None, :] == number[:, None]
    perm = jnp.sum(jnp.where(chosen, number[None, :], 0), axis=1)
    ordered = jnp.sum(jnp.where(chosen, flat[None, :], 0), axis=1)
    keep = jnp.concatenate([jnp.zeros((1,), jnp.int32), (ordered[1:] == ordered[:-1]).astype(jnp.int32)])
    column = jnp.arange(cols, dtype=jnp.int32)
    upto = jnp.sum((flat[None, :] <= column[:, None]).astype(jnp.int32), axis=1)
    own = jnp.sum((flat[None, :] == column[:, None]).astype(jnp.int32), axis=1)
    last = jnp.where(own > 0, upto - 1, blocks)
    source = jnp.where(flat < cols, flat, cols)
    hop = jnp.arange(hops, dtype=jnp.int32)
    reads = jnp.any(block_index[:, :, None] == (cols + hop)[None, None, :], axis=1)
    reads = jnp.sum(jnp.where(reads, 1 << hop, 0), axis=1)
    listed = jnp.sum(jnp.where(send_list[:, 0][None, :] == column[:, None], 1 << hop, 0), axis=1)
    parts = [source, perm, perm // neigh, keep, last, reads, listed, send_list.reshape(-1)]
    return jnp.concatenate(parts)


def kernel(
    sizes,
    tab, forcing_hbm, observed_hbm, jac_hbm, damping_hbm, error_weight_hbm, forcing_weight_hbm,
    traj_out, grad,
    forcing, observed, damping, error_weight, forcing_weight, load_sem, traj, misfit, subset, jac, xin, xb, halo, halo_out, adj, adj_b, sums, back, back_out, cin, cout,
    jac_sem, halo_send, halo_recv, hand_send, hand_recv,
    back_send, back_recv, cin_send, cin_recv,
):
    space, count = sizes
    steps, cols, members, lev = traj.shape
    neigh = jac[0].shape[0] // cols
    hops = halo.shape[1]
    blocks = cols * neigh
    at = Tables(cols, neigh, hops)
    me = lax.axis_index("space")
    turn = lax.axis_index("tm")
    is_first = turn == 0
    is_last = turn == count - 1
    group = cols // 2 if cols % 2 == 0 else cols
    tiles = 4 if blocks % 4 == 0 else 1
    half = blocks // tiles // 2 if blocks // tiles % 2 == 0 else blocks // tiles

    def place(distance, later):
        return {"space": lax.rem(me + distance + 2 * space, space), "tm": turn + later}

    def jac_copy(s):
        return pltpu.make_async_copy(jac_hbm.at[s], jac[s], jac_sem.at[s])

    def halo_copy(s, hop, later, landing):
        return pltpu.make_async_remote_copy(
            src_ref=halo_out.at[s, hop], dst_ref=halo.at[landing, hop],
            send_sem=halo_send.at[s, hop], recv_sem=halo_recv.at[landing, hop],
            device_id=place(OFFSETS[hop], later), device_id_type=MESH)

    def hand_copy():
        return pltpu.make_async_remote_copy(
            src_ref=traj.at[steps - 1], dst_ref=xin, send_sem=hand_send, recv_sem=hand_recv,
            device_id=place(0, 1), device_id_type=MESH)

    def back_copy(s, hop, later, landing):
        return pltpu.make_async_remote_copy(
            src_ref=back_out.at[s, hop], dst_ref=back.at[landing, hop],
            send_sem=back_send.at[s, hop], recv_sem=back_recv.at[landing, hop],
            device_id=place(-OFFSETS[hop], later), device_id_type=MESH)

    def cin_copy():
        return pltpu.make_async_remote_copy(
            src_ref=cout, dst_ref=cin, send_sem=cin_send, recv_sem=cin_recv,
            device_id=place(0, -1), device_id_type=MESH)

    @pl.when(jnp.logical_not(is_first))
    def _():
        jac_copy(0).start()

    for s in range(1, steps):
        jac_copy(s).start()

    loads = [
        pltpu.make_async_copy(source, target, load_sem.at[i])
        for i, (source, target) in enumerate([
            (forcing_hbm, forcing), (damping_hbm, damping), (observed_hbm, observed),
            (error_weight_hbm, error_weight), (forcing_weight_hbm, forcing_weight)])
    ]
    for load in loads:
        load.start()

    def rows(c):
        return pl.ds(c, members, stride=cols)

    barrier = pltpu.get_barrier_semaphore()

    def greet(later):
        for distance in OFFSETS + ((0,) if later else ()):
            pl.semaphore_signal(barrier, inc=1, device_id=place(distance, later), device_id_type=MESH)

    greet(0)

    @pl.when(jnp.logical_not(is_first))
    def _():
        greet(-1)

    @pl.when(jnp.logical_not(is_last))
    def _():
        greet(1)

    for s in range(steps):
        xb[s, cols] = jnp.zeros((ROWS, lev), BF16)
    sums[blocks] = jnp.zeros((members, lev), F32)
    sides = jnp.where(is_first, 0, 1) + jnp.where(is_last, 0, 1)
    pl.semaphore_wait(barrier, hops + sides * (hops + 1))

    def scalar(index):
        return tab[index].astype(F32)

    def subset_sums(terms):
        held = [jnp.zeros((members, lev), F32)]
        for term in terms:
            held = held + [term if i == 0 else value + term for i, value in enumerate(held)]
        for i, value in enumerate(held):
            subset[i] = value

    def advance(s, before):
        def some(g, carry):
            for i in range(group):
                c = g * group + i
                picked = [xb[s, tab[at.source + c * neigh + k]] for k in range(neigh)]
                held = [jac[s][c * neigh + k] for k in range(neigh)]
                turned = lax.dot_general(
                    jnp.concatenate(held, axis=1), jnp.concatenate(picked, axis=1),
                    (((1,), (1,)), ((), ())), preferred_element_type=F32)
                mixed = jnp.transpose(turned)[:members]
                damp = damping[pl.ds(c, 1), :]
                traj[s, c] = damp * before[c] + forcing[s, rows(c), :] + mixed
            return carry

        lax.fori_loop(0, cols // group, some, 0)
        remote = []
        for hop in range(hops):
            halo_copy(0, hop, 0, s).wait_recv()
        for hop in range(hops):
            block = tab[at.perm + blocks - hops + hop]
            remote.append(lax.dot_general(
                halo[s, hop], jac[s][block], (((1,), (1,)), ((), ())),
                preferred_element_type=F32)[:members])
        subset_sums(remote)
        for hop in range(hops):
            c = tab[at.send + hop]
            value = traj[s, c] + subset[tab[at.reads + c]]
            halo_out[s, hop, 0:members] = value.astype(BF16)
        send_listed(s)
        for c in range(cols):
            value = traj[s, c] + subset[tab[at.reads + c]]
            traj[s, c] = value
            if s < steps - 1:
                xb[s + 1, c, 0:members] = value.astype(BF16)

    def send_listed(s):
        if s < steps - 1:
            for hop in range(hops):
                halo_copy(s, hop, 0, s + 1).start()
        else:
            @pl.when(jnp.logical_not(is_last))
            def _():
                for hop in range(hops):
                    halo_copy(s, hop, 1, 0).start()

    def hand_on(s):
        if s == steps - 1:
            @pl.when(jnp.logical_not(is_last))
            def _():
                hand_copy().start()

    for load in loads[:2]:
        load.wait()

    @pl.when(is_first)
    def _():
        for hop in range(hops):
            halo_out[0, hop, 0:members] = forcing[0, rows(tab[at.send + hop]), :].astype(BF16)
        send_listed(0)
        for c in range(cols):
            value = forcing[0, rows(c), :]
            traj[0, c] = value
            if steps > 1:
                xb[1, c, 0:members] = value.astype(BF16)

    @pl.when(jnp.logical_not(is_first))
    def _():
        jac_copy(0).wait()
        hand_copy().wait_recv()
        for c in range(cols):
            xb[0, c, 0:members] = xin[c].astype(BF16)
        advance(0, xin)

    hand_on(0)
    for s in range(1, steps):
        jac_copy(s).wait()
        advance(s, traj.at[s - 1])
        hand_on(s)

    for load in loads[2:]:
        load.wait()
    for s in range(steps):
        for c in range(cols):
            misfit[s, c] = error_weight[pl.ds(c, 1), :] * (traj[s, c] - observed[s, rows(c), :])
            traj_out[s, rows(c), :] = traj[s, c]

    def add_back(landing):
        subset_sums([back[landing, hop] for hop in range(hops)])

    def transpose_borders(s, value_of):
        for hop in range(hops):
            spot = blocks - hops + hop
            value = value_of(tab[at.column + spot]).astype(BF16)
            back_out[s, hop] = jnp.dot(
                value, jac[s][tab[at.perm + spot]], preferred_element_type=F32)
            if s > 0:
                back_copy(s, hop, 0, s - 1).start()
            else:
                back_copy(s, hop, -1, steps - 1).start()

    def keep_adjoint(s, value_of):
        for c in range(cols):
            value = value_of(c)
            adj[s, c] = value
            adj_b[c, 0:members] = value.astype(BF16)

    def own_part(s, c):
        return damping[pl.ds(c, 1), :] * adj[s, c] + sums[tab[at.last + c]]

    def transpose_step(s):
        blank = jnp.zeros((ROWS, lev), BF16)

        def some(g, total):
            for i in range(half):
                first = (g * half + i) * tiles
                turned = [adj_b[tab[at.column + first + n]] for n in range(tiles)]
                held = [jac[s][tab[at.perm + first + n]] for n in range(tiles)]
                if tiles == 4:
                    left = [jnp.concatenate([w, blank], axis=1) for w in turned[:2]]
                    left += [jnp.concatenate([blank, w], axis=1) for w in turned[2:]]
                    left = jnp.concatenate(left, axis=0)
                    upper = jnp.concatenate(held[:2], axis=1)
                    lower = jnp.concatenate(held[2:], axis=1)
                    right = jnp.concatenate([upper, lower], axis=0)
                else:
                    left, right = turned[0], held[0]
                spread = jnp.dot(left, right, preferred_element_type=F32)
                for n in range(tiles):
                    lane = n % 2 * lev
                    part = spread[n * ROWS : n * ROWS + members, lane : lane + lev]
                    total = part + scalar(at.keep + first + n) * total
                    sums[first + n] = total
            return total

        lax.fori_loop(0, blocks // tiles // half, some, jnp.zeros((members, lev), F32))

    top = steps - 1

    @pl.when(is_last)
    def _():
        def value_of(c):
            return misfit[top, c]

        if top > 0:
            transpose_borders(top, value_of)
        keep_adjoint(top, value_of)

    @pl.when(jnp.logical_not(is_last))
    def _():
        for hop in range(hops):
            back_copy(0, hop, 0, top).wait_recv()
        add_back(top)
        cin_copy().wait_recv()

        def value_of(c):
            return misfit[top, c] + cin[c] + subset[tab[at.listed + c]]

        if top > 0:
            transpose_borders(top, value_of)
        keep_adjoint(top, value_of)

    for s in range(top, 0, -1):
        transpose_step(s)
        for hop in range(hops):
            back_copy(0, hop, 0, s - 1).wait_recv()
        add_back(s - 1)

        def value_of(c, s=s):
            return misfit[s - 1, c] + own_part(s, c) + subset[tab[at.listed + c]]

        if s > 1:
            transpose_borders(s - 1, value_of)
        else:
            @pl.when(jnp.logical_not(is_first))
            def _():
                transpose_borders(0, value_of)

        keep_adjoint(s - 1, value_of)

    @pl.when(jnp.logical_not(is_first))
    def _():
        transpose_step(0)
        for c in range(cols):
            cout[c] = own_part(0, c)
        cin_copy().start()

    for s in range(steps):
        for c in range(cols):
            grad[s, rows(c), :] = forcing_weight[...] * forcing[s, rows(c), :] + adj[s, c]

    @pl.when(jnp.logical_not(is_first))
    def _():
        for hop in range(hops):
            back_copy(0, hop, -1, steps - 1).wait_send()
        cin_copy().wait_send()

    for s in range(1, steps):
        for hop in range(hops):
            back_copy(s, hop, 0, s - 1).wait_send()
            halo_copy(s - 1, hop, 0, s).wait_send()

    @pl.when(jnp.logical_not(is_last))
    def _():
        for hop in range(hops):
            halo_copy(steps - 1, hop, 1, 0).wait_send()
        hand_copy().wait_send()


def copy_kernel(first_in, second_in, first_out, second_out, sem):
    first = pltpu.make_async_copy(first_in, first_out, sem.at[0])
    second = pltpu.make_async_copy(second_in, second_out, sem.at[1])
    first.start()
    second.start()
    first.wait()
    second.wait()


def on_device(
    sizes, forcing, observed, jacobian, block_index, send_list, damping, error_weight, forcing_weight
):
    steps, cols, members, lev = forcing.shape
    neigh = jacobian.shape[2]
    hops = send_list.shape[0]
    blocks = cols * neigh
    tab = index_tables(block_index, send_list)
    vmem = pl.BlockSpec(memory_space=pltpu.VMEM)
    far = pl.BlockSpec(memory_space=pl.ANY)
    flat = (steps, members * cols, lev)

    def by_member(array):
        return array.transpose(0, 2, 1, 3).reshape(flat)

    def by_column(array):
        return array.reshape(steps, members, cols, lev).transpose(0, 2, 1, 3)

    state = (cols, members, lev)
    dma = pltpu.SemaphoreType.DMA
    trajectory, gradient = pl.pallas_call(
        functools.partial(kernel, sizes),
        out_shape=(jax.ShapeDtypeStruct(flat, F32),) * 2,
        in_specs=[pl.BlockSpec(memory_space=pltpu.SMEM)] + [far] * 6,
        out_specs=(vmem, vmem),
        scratch_shapes=[
            pltpu.VMEM(flat, F32), pltpu.VMEM(flat, F32),
            pltpu.VMEM((cols, lev), F32), pltpu.VMEM((cols, lev), F32), pltpu.VMEM((1, lev), F32),
            dma((5,)),
            pltpu.VMEM(forcing.shape, F32),
            pltpu.VMEM(forcing.shape, F32),
            pltpu.VMEM((2 ** hops, members, lev), F32),
            [pltpu.VMEM((blocks, lev, lev), BF16) for _ in range(steps)],
            pltpu.VMEM(state, F32),
            pltpu.VMEM((steps, cols + 1, ROWS, lev), BF16),
            pltpu.VMEM((steps, hops, ROWS, lev), BF16),
            pltpu.VMEM((steps, hops, ROWS, lev), BF16),
            pltpu.VMEM(forcing.shape, F32),
            pltpu.VMEM((cols, ROWS, lev), BF16),
            pltpu.VMEM((blocks + 1, members, lev), F32),
            pltpu.VMEM((steps, hops, members, lev), F32),
            pltpu.VMEM((steps, hops, members, lev), F32),
            pltpu.VMEM(state, F32),
            pltpu.VMEM(state, F32),
            dma((steps,)),
            dma((steps, hops)), dma((steps, hops)), dma(()), dma(()),
            dma((steps, hops)), dma((steps, hops)), dma(()), dma(()),
        ],
        compiler_params=pltpu.CompilerParams(
            collective_id=0, has_side_effects=True, vmem_limit_bytes=63 * 1024 * 1024),
    )(
        tab, by_member(forcing), by_member(observed), jacobian.reshape(steps, blocks, lev, lev),
        damping, error_weight, forcing_weight.reshape(1, lev),
    )
    trajectory, gradient = pl.pallas_call(
        copy_kernel,
        out_shape=(jax.ShapeDtypeStruct(flat, F32),) * 2,
        in_specs=[far, far],
        out_specs=(far, far),
        scratch_shapes=[dma((2,))],
        compiler_params=pltpu.CompilerParams(vmem_limit_bytes=63 * 1024 * 1024),
    )(trajectory, gradient)
    return by_column(trajectory), by_column(gradient)


def solution(mesh):
    sizes = (mesh.shape["space"], mesh.shape["tm"])
    in_specs = (
        P("tm", "space", None, None),
        P("tm", "space", None, None),
        P("tm", "space", None, None, None),
        P("space", None),
        P("space", None),
        P("space", None),
        P("space", None),
        P(),
    )
    out_specs = (P("tm", "space", None, None), P("tm", "space", None, None))
    return jax.shard_map(
        functools.partial(on_device, sizes), mesh=mesh, in_specs=in_specs, out_specs=out_specs,
        check_vma=False,
    )
```

```python
import functools
import jax
import jax.numpy as jnp
from jax import lax
from jax.experimental import pallas as pl
from jax.experimental.pallas import tpu as pltpu
from jax.sharding import PartitionSpec as P

OFFSETS = (1, -1, 2, -2)
ROWS = 32
MESH = pl.DeviceIdType.MESH
F32 = jnp.float32
BF16 = jnp.bfloat16


class Tables:
    def __init__(self, cols, neigh, hops):
        blocks = cols * neigh
        self.source = 0
        self.perm = self.source + blocks
        self.column = self.perm + blocks
        self.keep = self.column + blocks
        self.last = self.keep + blocks
        self.reads = self.last + cols
        self.listed = self.reads + cols
        self.send = self.listed + cols


def index_tables(block_index, send_list):
    cols, neigh = block_index.shape
    hops = send_list.shape[0]
    blocks = cols * neigh
    flat = block_index.reshape(-1)
    number = jnp.arange(blocks, dtype=jnp.int32)
    key = flat * blocks + number
    rank = jnp.sum((key[None, :] < key[:, None]).astype(jnp.int32), axis=1)
    chosen = rank[None, :] == number[:, None]
    perm = jnp.sum(jnp.where(chosen, number[None, :], 0), axis=1)
    ordered = jnp.sum(jnp.where(chosen, flat[None, :], 0), axis=1)
    keep = jnp.concatenate([jnp.zeros((1,), jnp.int32), (ordered[1:] == ordered[:-1]).astype(jnp.int32)])
    column = jnp.arange(cols, dtype=jnp.int32)
    upto = jnp.sum((flat[None, :] <= column[:, None]).astype(jnp.int32), axis=1)
    own = jnp.sum((flat[None, :] == column[:, None]).astype(jnp.int32), axis=1)
    last = jnp.where(own > 0, upto - 1, blocks)
    source = jnp.where(flat < cols, flat, cols)
    hop = jnp.arange(hops, dtype=jnp.int32)
    reads = jnp.any(block_index[:, :, None] == (cols + hop)[None, None, :], axis=1)
    reads = jnp.sum(jnp.where(reads, 1 << hop, 0), axis=1)
    listed = jnp.sum(jnp.where(send_list[:, 0][None, :] == column[:, None], 1 << hop, 0), axis=1)
    parts = [source, perm, perm // neigh, keep, last, reads, listed, send_list.reshape(-1)]
    return jnp.concatenate(parts)


def kernel(
    sizes,
    tab, forcing_hbm, observed_hbm, jac_hbm, damping_hbm, error_weight_hbm, forcing_weight_hbm,
    traj_out, grad,
    forcing, observed, damping, error_weight, forcing_weight, load_sem, traj, misfit, subset, jac, xin, xb, halo, halo_out, adj, adj_b, sums, back, back_out, cin, cout,
    jac_sem, halo_send, halo_recv, hand_send, hand_recv,
    back_send, back_recv, cin_send, cin_recv,
):
    space, count = sizes
    steps, cols, members, lev = traj.shape
    neigh = jac[0].shape[0] // cols
    hops = halo.shape[1]
    blocks = cols * neigh
    at = Tables(cols, neigh, hops)
    me = lax.axis_index("space")
    turn = lax.axis_index("tm")
    is_first = turn == 0
    is_last = turn == count - 1
    stack = 4 if cols % 4 == 0 else 1
    group = cols // stack // 2 if cols // stack % 2 == 0 else cols // stack
    tiles = 4 if blocks % 4 == 0 else 1
    half = blocks // tiles // 2 if blocks // tiles % 2 == 0 else blocks // tiles

    def place(distance, later):
        return {"space": lax.rem(me + distance + 2 * space, space), "tm": turn + later}

    def jac_copy(s):
        return pltpu.make_async_copy(jac_hbm.at[s], jac[s], jac_sem.at[s])

    def halo_copy(s, hop, later, landing):
        return pltpu.make_async_remote_copy(
            src_ref=halo_out.at[s, hop], dst_ref=halo.at[landing, hop],
            send_sem=halo_send.at[s, hop], recv_sem=halo_recv.at[landing, hop],
            device_id=place(OFFSETS[hop], later), device_id_type=MESH)

    def hand_copy():
        return pltpu.make_async_remote_copy(
            src_ref=traj.at[steps - 1], dst_ref=xin, send_sem=hand_send, recv_sem=hand_recv,
            device_id=place(0, 1), device_id_type=MESH)

    def back_copy(s, hop, later, landing):
        return pltpu.make_async_remote_copy(
            src_ref=back_out.at[s, hop], dst_ref=back.at[landing, hop],
            send_sem=back_send.at[s, hop], recv_sem=back_recv.at[landing, hop],
            device_id=place(-OFFSETS[hop], later), device_id_type=MESH)

    def cin_copy():
        return pltpu.make_async_remote_copy(
            src_ref=cout, dst_ref=cin, send_sem=cin_send, recv_sem=cin_recv,
            device_id=place(0, -1), device_id_type=MESH)

    @pl.when(jnp.logical_not(is_first))
    def _():
        jac_copy(0).start()

    for s in range(1, steps):
        jac_copy(s).start()

    loads = [
        pltpu.make_async_copy(source, target, load_sem.at[i])
        for i, (source, target) in enumerate([
            (forcing_hbm, forcing), (damping_hbm, damping), (observed_hbm, observed),
            (error_weight_hbm, error_weight), (forcing_weight_hbm, forcing_weight)])
    ]
    for load in loads:
        load.start()

    def rows(c):
        return pl.ds(c, members, stride=cols)

    barrier = pltpu.get_barrier_semaphore()

    def greet(later):
        for distance in OFFSETS + ((0,) if later else ()):
            pl.semaphore_signal(barrier, inc=1, device_id=place(distance, later), device_id_type=MESH)

    greet(0)

    @pl.when(jnp.logical_not(is_first))
    def _():
        greet(-1)

    @pl.when(jnp.logical_not(is_last))
    def _():
        greet(1)

    for s in range(steps):
        xb[s, cols] = jnp.zeros((ROWS, lev), BF16)
    sums[blocks] = jnp.zeros((members, lev), F32)
    sides = jnp.where(is_first, 0, 1) + jnp.where(is_last, 0, 1)
    pl.semaphore_wait(barrier, hops + sides * (hops + 1))

    def scalar(index):
        return tab[index].astype(F32)

    def subset_sums(terms):
        held = [jnp.zeros((members, lev), F32)]
        for term in terms:
            held = held + [term if i == 0 else value + term for i, value in enumerate(held)]
        for i, value in enumerate(held):
            subset[i] = value

    def advance(s, before):
        lanes = lax.broadcasted_iota(jnp.int32, (lev, stack * ROWS), 1) // ROWS

        def some(g, carry):
            for i in range(group):
                first = (g * group + i) * stack
                left, right = [], []
                for r in range(stack):
                    here = (first + r) * neigh
                    left.append(jnp.concatenate([jac[s][here + k] for k in range(neigh)], axis=1))
                    right.append(jnp.concatenate([xb[s, tab[at.source + here + k]] for k in range(neigh)], axis=1))
                turned = lax.dot_general(
                    jnp.concatenate(left, axis=0), jnp.concatenate(right, axis=0),
                    (((1,), (1,)), ((), ())), preferred_element_type=F32)
                chosen = turned[:lev]
                for r in range(1, stack):
                    chosen = jnp.where(lanes == r, turned[r * lev : (r + 1) * lev], chosen)
                mixed = jnp.transpose(chosen)
                for r in range(stack):
                    c = first + r
                    damp = damping[pl.ds(c, 1), :]
                    own = mixed[r * ROWS : r * ROWS + members]
                    traj[s, c] = damp * before[c] + forcing[s, rows(c), :] + own
            return carry

        lax.fori_loop(0, cols // stack // group, some, 0)
        remote = []
        for hop in range(hops):
            halo_copy(0, hop, 0, s).wait_recv()
        for hop in range(hops):
            block = tab[at.perm + blocks - hops + hop]
            remote.append(lax.dot_general(
                halo[s, hop], jac[s][block], (((1,), (1,)), ((), ())),
                preferred_element_type=F32)[:members])
        subset_sums(remote)
        for hop in range(hops):
            c = tab[at.send + hop]
            value = traj[s, c] + subset[tab[at.reads + c]]
            halo_out[s, hop, 0:members] = value.astype(BF16)
        send_listed(s)
        for c in range(cols):
            value = traj[s, c] + subset[tab[at.reads + c]]
            traj[s, c] = value
            if s < steps - 1:
                xb[s + 1, c, 0:members] = value.astype(BF16)

    def send_listed(s):
        if s < steps - 1:
            for hop in range(hops):
                halo_copy(s, hop, 0, s + 1).start()
        else:
            @pl.when(jnp.logical_not(is_last))
            def _():
                for hop in range(hops):
                    halo_copy(s, hop, 1, 0).start()

    def hand_on(s):
        if s == steps - 1:
            @pl.when(jnp.logical_not(is_last))
            def _():
                hand_copy().start()

    for load in loads[:2]:
        load.wait()

    @pl.when(is_first)
    def _():
        for hop in range(hops):
            halo_out[0, hop, 0:members] = forcing[0, rows(tab[at.send + hop]), :].astype(BF16)
        send_listed(0)
        for c in range(cols):
            value = forcing[0, rows(c), :]
            traj[0, c] = value
            if steps > 1:
                xb[1, c, 0:members] = value.astype(BF16)

    @pl.when(jnp.logical_not(is_first))
    def _():
        jac_copy(0).wait()
        hand_copy().wait_recv()
        for c in range(cols):
            xb[0, c, 0:members] = xin[c].astype(BF16)
        advance(0, xin)

    hand_on(0)
    for s in range(1, steps):
        jac_copy(s).wait()
        advance(s, traj.at[s - 1])
        hand_on(s)

    for load in loads[2:]:
        load.wait()
    for s in range(steps):
        for c in range(cols):
            misfit[s, c] = error_weight[pl.ds(c, 1), :] * (traj[s, c] - observed[s, rows(c), :])
            traj_out[s, rows(c), :] = traj[s, c]

    def add_back(landing):
        subset_sums([back[landing, hop] for hop in range(hops)])

    def transpose_borders(s, value_of):
        for hop in range(hops):
            spot = blocks - hops + hop
            value = value_of(tab[at.column + spot]).astype(BF16)
            back_out[s, hop] = jnp.dot(
                value, jac[s][tab[at.perm + spot]], preferred_element_type=F32)
            if s > 0:
                back_copy(s, hop, 0, s - 1).start()
            else:
                back_copy(s, hop, -1, steps - 1).start()

    def keep_adjoint(s, value_of):
        for c in range(cols):
            value = value_of(c)
            adj[s, c] = value
            adj_b[c, 0:members] = value.astype(BF16)

    def own_part(s, c):
        return damping[pl.ds(c, 1), :] * adj[s, c] + sums[tab[at.last + c]]

    def transpose_step(s):
        blank = jnp.zeros((ROWS, lev), BF16)

        def some(g, total):
            for i in range(half):
                first = (g * half + i) * tiles
                turned = [adj_b[tab[at.column + first + n]] for n in range(tiles)]
                held = [jac[s][tab[at.perm + first + n]] for n in range(tiles)]
                if tiles == 4:
                    left = [jnp.concatenate([w, blank], axis=1) for w in turned[:2]]
                    left += [jnp.concatenate([blank, w], axis=1) for w in turned[2:]]
                    left = jnp.concatenate(left, axis=0)
                    upper = jnp.concatenate(held[:2], axis=1)
                    lower = jnp.concatenate(held[2:], axis=1)
                    right = jnp.concatenate([upper, lower], axis=0)
                else:
                    left, right = turned[0], held[0]
                spread = jnp.dot(left, right, preferred_element_type=F32)
                for n in range(tiles):
                    lane = n % 2 * lev
                    part = spread[n * ROWS : n * ROWS + members, lane : lane + lev]
                    total = part + scalar(at.keep + first + n) * total
                    sums[first + n] = total
            return total

        lax.fori_loop(0, blocks // tiles // half, some, jnp.zeros((members, lev), F32))

    top = steps - 1

    @pl.when(is_last)
    def _():
        def value_of(c):
            return misfit[top, c]

        if top > 0:
            transpose_borders(top, value_of)
        keep_adjoint(top, value_of)

    @pl.when(jnp.logical_not(is_last))
    def _():
        for hop in range(hops):
            back_copy(0, hop, 0, top).wait_recv()
        add_back(top)
        cin_copy().wait_recv()

        def value_of(c):
            return misfit[top, c] + cin[c] + subset[tab[at.listed + c]]

        if top > 0:
            transpose_borders(top, value_of)
        keep_adjoint(top, value_of)

    for s in range(top, 0, -1):
        transpose_step(s)
        for hop in range(hops):
            back_copy(0, hop, 0, s - 1).wait_recv()
        add_back(s - 1)

        def value_of(c, s=s):
            return misfit[s - 1, c] + own_part(s, c) + subset[tab[at.listed + c]]

        if s > 1:
            transpose_borders(s - 1, value_of)
        else:
            @pl.when(jnp.logical_not(is_first))
            def _():
                transpose_borders(0, value_of)

        keep_adjoint(s - 1, value_of)

    @pl.when(jnp.logical_not(is_first))
    def _():
        transpose_step(0)
        for c in range(cols):
            cout[c] = own_part(0, c)
        cin_copy().start()

    for s in range(steps):
        for c in range(cols):
            grad[s, rows(c), :] = forcing_weight[...] * forcing[s, rows(c), :] + adj[s, c]

    @pl.when(jnp.logical_not(is_first))
    def _():
        for hop in range(hops):
            back_copy(0, hop, -1, steps - 1).wait_send()
        cin_copy().wait_send()

    for s in range(1, steps):
        for hop in range(hops):
            back_copy(s, hop, 0, s - 1).wait_send()
            halo_copy(s - 1, hop, 0, s).wait_send()

    @pl.when(jnp.logical_not(is_last))
    def _():
        for hop in range(hops):
            halo_copy(steps - 1, hop, 1, 0).wait_send()
        hand_copy().wait_send()


def copy_kernel(first_in, second_in, first_out, second_out, first, second, sem):
    loads = [
        pltpu.make_async_copy(first_in, first, sem.at[0]),
        pltpu.make_async_copy(second_in, second, sem.at[1]),
    ]
    stores = [
        pltpu.make_async_copy(first, first_out, sem.at[2]),
        pltpu.make_async_copy(second, second_out, sem.at[3]),
    ]
    for load in loads:
        load.start()
    for load, store in zip(loads, stores):
        load.wait()
        store.start()
    for store in stores:
        store.wait()


def on_device(
    sizes, forcing, observed, jacobian, block_index, send_list, damping, error_weight, forcing_weight
):
    steps, cols, members, lev = forcing.shape
    neigh = jacobian.shape[2]
    hops = send_list.shape[0]
    blocks = cols * neigh
    tab = index_tables(block_index, send_list)
    vmem = pl.BlockSpec(memory_space=pltpu.VMEM)
    far = pl.BlockSpec(memory_space=pl.ANY)
    flat = (steps, members * cols, lev)

    def by_member(array):
        return array.transpose(0, 2, 1, 3).reshape(flat)

    def by_column(array):
        return array.reshape(steps, members, cols, lev).transpose(0, 2, 1, 3)

    state = (cols, members, lev)
    dma = pltpu.SemaphoreType.DMA
    trajectory, gradient = pl.pallas_call(
        functools.partial(kernel, sizes),
        out_shape=(jax.ShapeDtypeStruct(flat, F32),) * 2,
        in_specs=[pl.BlockSpec(memory_space=pltpu.SMEM)] + [far] * 6,
        out_specs=(vmem, vmem),
        scratch_shapes=[
            pltpu.VMEM(flat, F32), pltpu.VMEM(flat, F32),
            pltpu.VMEM((cols, lev), F32), pltpu.VMEM((cols, lev), F32), pltpu.VMEM((1, lev), F32),
            dma((5,)),
            pltpu.VMEM(forcing.shape, F32),
            pltpu.VMEM(forcing.shape, F32),
            pltpu.VMEM((2 ** hops, members, lev), F32),
            [pltpu.VMEM((blocks, lev, lev), BF16) for _ in range(steps)],
            pltpu.VMEM(state, F32),
            pltpu.VMEM((steps, cols + 1, ROWS, lev), BF16),
            pltpu.VMEM((steps, hops, ROWS, lev), BF16),
            pltpu.VMEM((steps, hops, ROWS, lev), BF16),
            pltpu.VMEM(forcing.shape, F32),
            pltpu.VMEM((cols, ROWS, lev), BF16),
            pltpu.VMEM((blocks + 1, members, lev), F32),
            pltpu.VMEM((steps, hops, members, lev), F32),
            pltpu.VMEM((steps, hops, members, lev), F32),
            pltpu.VMEM(state, F32),
            pltpu.VMEM(state, F32),
            dma((steps,)),
            dma((steps, hops)), dma((steps, hops)), dma(()), dma(()),
            dma((steps, hops)), dma((steps, hops)), dma(()), dma(()),
        ],
        compiler_params=pltpu.CompilerParams(
            collective_id=0, has_side_effects=True, vmem_limit_bytes=63 * 1024 * 1024),
    )(
        tab, by_member(forcing), by_member(observed), jacobian.reshape(steps, blocks, lev, lev),
        damping, error_weight, forcing_weight.reshape(1, lev),
    )
    trajectory, gradient = pl.pallas_call(
        copy_kernel,
        out_shape=(jax.ShapeDtypeStruct(flat, F32),) * 2,
        in_specs=[far, far],
        out_specs=(far, far),
        scratch_shapes=[pltpu.VMEM(flat, F32), pltpu.VMEM(flat, F32), dma((4,))],
        compiler_params=pltpu.CompilerParams(vmem_limit_bytes=63 * 1024 * 1024),
    )(trajectory, gradient)
    return by_column(trajectory), by_column(gradient)


def solution(mesh):
    sizes = (mesh.shape["space"], mesh.shape["tm"])
    in_specs = (
        P("tm", "space", None, None),
        P("tm", "space", None, None),
        P("tm", "space", None, None, None),
        P("space", None),
        P("space", None),
        P("space", None),
        P("space", None),
        P(),
    )
    out_specs = (P("tm", "space", None, None), P("tm", "space", None, None))
    return jax.shard_map(
        functools.partial(on_device, sizes), mesh=mesh, in_specs=in_specs, out_specs=out_specs,
        check_vma=False,
    )
```

```python
import functools
import jax
import jax.numpy as jnp
from jax import lax
from jax.experimental import pallas as pl
from jax.experimental.pallas import tpu as pltpu
from jax.sharding import PartitionSpec as P

OFFSETS = (1, -1, 2, -2)
ROWS = 32
MESH = pl.DeviceIdType.MESH
F32 = jnp.float32
BF16 = jnp.bfloat16


class Tables:
    def __init__(self, cols, neigh, hops):
        blocks = cols * neigh
        self.source = 0
        self.perm = self.source + blocks
        self.column = self.perm + blocks
        self.keep = self.column + blocks
        self.last = self.keep + blocks
        self.reads = self.last + cols
        self.listed = self.reads + cols
        self.send = self.listed + cols


def index_tables(block_index, send_list):
    cols, neigh = block_index.shape
    hops = send_list.shape[0]
    blocks = cols * neigh
    flat = block_index.reshape(-1)
    number = jnp.arange(blocks, dtype=jnp.int32)
    key = flat * blocks + number
    rank = jnp.sum((key[None, :] < key[:, None]).astype(jnp.int32), axis=1)
    chosen = rank[None, :] == number[:, None]
    perm = jnp.sum(jnp.where(chosen, number[None, :], 0), axis=1)
    ordered = jnp.sum(jnp.where(chosen, flat[None, :], 0), axis=1)
    keep = jnp.concatenate([jnp.zeros((1,), jnp.int32), (ordered[1:] == ordered[:-1]).astype(jnp.int32)])
    column = jnp.arange(cols, dtype=jnp.int32)
    upto = jnp.sum((flat[None, :] <= column[:, None]).astype(jnp.int32), axis=1)
    own = jnp.sum((flat[None, :] == column[:, None]).astype(jnp.int32), axis=1)
    last = jnp.where(own > 0, upto - 1, blocks)
    source = jnp.where(flat < cols, flat, cols)
    hop = jnp.arange(hops, dtype=jnp.int32)
    reads = jnp.any(block_index[:, :, None] == (cols + hop)[None, None, :], axis=1)
    reads = jnp.sum(jnp.where(reads, 1 << hop, 0), axis=1)
    listed = jnp.sum(jnp.where(send_list[:, 0][None, :] == column[:, None], 1 << hop, 0), axis=1)
    parts = [source, perm, perm // neigh, keep, last, reads, listed, send_list.reshape(-1)]
    return jnp.concatenate(parts)


def kernel(
    sizes,
    tab, forcing_hbm, observed_hbm, jac_hbm, damping_hbm, error_weight_hbm, forcing_weight_hbm,
    traj_out, grad,
    forcing, observed, damping, error_weight, forcing_weight, load_sem, traj, misfit, subset, part, fix_out, fix_in, fix_send, fix_recv, jac, xin, xb, halo, halo_out, adj, adj_b, sums, back, back_out, cin, cout,
    jac_sem, halo_send, halo_recv, hand_send, hand_recv,
    back_send, back_recv, cin_send, cin_recv,
):
    space, count = sizes
    steps, cols, members, lev = traj.shape
    neigh = jac[0].shape[0] // cols
    hops = halo.shape[1]
    blocks = cols * neigh
    at = Tables(cols, neigh, hops)
    me = lax.axis_index("space")
    turn = lax.axis_index("tm")
    is_first = turn == 0
    is_last = turn == count - 1
    stack = 4 if cols % 4 == 0 else 1
    group = cols // stack // 2 if cols // stack % 2 == 0 else cols // stack
    tiles = 4 if blocks % 4 == 0 else 1
    half = blocks // tiles // 2 if blocks // tiles % 2 == 0 else blocks // tiles

    def place(distance, later):
        return {"space": lax.rem(me + distance + 2 * space, space), "tm": turn + later}

    def jac_copy(s):
        return pltpu.make_async_copy(jac_hbm.at[s], jac[s], jac_sem.at[s])

    def halo_copy(s, hop, later, landing):
        return pltpu.make_async_remote_copy(
            src_ref=halo_out.at[s, hop], dst_ref=halo.at[landing, hop],
            send_sem=halo_send.at[s, hop], recv_sem=halo_recv.at[landing, hop],
            device_id=place(OFFSETS[hop], later), device_id_type=MESH)

    def hand_copy():
        return pltpu.make_async_remote_copy(
            src_ref=part, dst_ref=xin, send_sem=hand_send, recv_sem=hand_recv,
            device_id=place(0, 1), device_id_type=MESH)

    def fix_copy():
        return pltpu.make_async_remote_copy(
            src_ref=fix_out, dst_ref=fix_in, send_sem=fix_send, recv_sem=fix_recv,
            device_id=place(0, 1), device_id_type=MESH)

    def back_copy(s, hop, later, landing):
        return pltpu.make_async_remote_copy(
            src_ref=back_out.at[s, hop], dst_ref=back.at[landing, hop],
            send_sem=back_send.at[s, hop], recv_sem=back_recv.at[landing, hop],
            device_id=place(-OFFSETS[hop], later), device_id_type=MESH)

    def cin_copy():
        return pltpu.make_async_remote_copy(
            src_ref=cout, dst_ref=cin, send_sem=cin_send, recv_sem=cin_recv,
            device_id=place(0, -1), device_id_type=MESH)

    @pl.when(jnp.logical_not(is_first))
    def _():
        jac_copy(0).start()

    for s in range(1, steps):
        jac_copy(s).start()

    loads = [
        pltpu.make_async_copy(source, target, load_sem.at[i])
        for i, (source, target) in enumerate([
            (forcing_hbm, forcing), (damping_hbm, damping), (observed_hbm, observed),
            (error_weight_hbm, error_weight), (forcing_weight_hbm, forcing_weight)])
    ]
    for load in loads:
        load.start()

    def rows(c):
        return pl.ds(c, members, stride=cols)

    barrier = pltpu.get_barrier_semaphore()

    def greet(later):
        for distance in OFFSETS + ((0,) if later else ()):
            pl.semaphore_signal(barrier, inc=1, device_id=place(distance, later), device_id_type=MESH)

    greet(0)

    @pl.when(jnp.logical_not(is_first))
    def _():
        greet(-1)

    @pl.when(jnp.logical_not(is_last))
    def _():
        greet(1)

    for s in range(steps):
        xb[s, cols] = jnp.zeros((ROWS, lev), BF16)
    sums[blocks] = jnp.zeros((members, lev), F32)
    sides = jnp.where(is_first, 0, 1) + jnp.where(is_last, 0, 1)
    pl.semaphore_wait(barrier, hops + sides * (hops + 1))

    def scalar(index):
        return tab[index].astype(F32)

    def subset_sums(terms):
        held = [jnp.zeros((members, lev), F32)]
        for term in terms:
            held = held + [term if i == 0 else value + term for i, value in enumerate(held)]
        for i, value in enumerate(held):
            subset[i] = value

    def advance(s, before):
        lanes = lax.broadcasted_iota(jnp.int32, (lev, stack * ROWS), 1) // ROWS

        def some(g, carry):
            for i in range(group):
                first = (g * group + i) * stack
                left, right = [], []
                for r in range(stack):
                    here = (first + r) * neigh
                    left.append(jnp.concatenate([jac[s][here + k] for k in range(neigh)], axis=1))
                    right.append(jnp.concatenate([xb[s, tab[at.source + here + k]] for k in range(neigh)], axis=1))
                turned = lax.dot_general(
                    jnp.concatenate(left, axis=0), jnp.concatenate(right, axis=0),
                    (((1,), (1,)), ((), ())), preferred_element_type=F32)
                chosen = turned[:lev]
                for r in range(1, stack):
                    chosen = jnp.where(lanes == r, turned[r * lev : (r + 1) * lev], chosen)
                mixed = jnp.transpose(chosen)
                for r in range(stack):
                    c = first + r
                    damp = damping[pl.ds(c, 1), :]
                    own = mixed[r * ROWS : r * ROWS + members]
                    part[c] = damp * before[c] + forcing[s, rows(c), :] + own
            return carry

        lax.fori_loop(0, cols // stack // group, some, 0)
        hand_on(s)
        remote = []
        for hop in range(hops):
            halo_copy(0, hop, 0, s).wait_recv()
        for hop in range(hops):
            block = tab[at.perm + blocks - hops + hop]
            remote.append(lax.dot_general(
                halo[s, hop], jac[s][block], (((1,), (1,)), ((), ())),
                preferred_element_type=F32)[:members])
        if s == steps - 1:
            for hop in range(hops):
                fix_out[hop] = remote[hop]

            @pl.when(jnp.logical_not(is_last))
            def _():
                fix_copy().start()

        subset_sums(remote)
        for hop in range(hops):
            c = tab[at.send + hop]
            value = part[c] + subset[tab[at.reads + c]]
            halo_out[s, hop, 0:members] = value.astype(BF16)
        send_listed(s)
        for c in range(cols):
            value = part[c] + subset[tab[at.reads + c]]
            traj[s, c] = value
            if s < steps - 1:
                xb[s + 1, c, 0:members] = value.astype(BF16)

    def send_listed(s):
        if s < steps - 1:
            for hop in range(hops):
                halo_copy(s, hop, 0, s + 1).start()
        else:
            @pl.when(jnp.logical_not(is_last))
            def _():
                for hop in range(hops):
                    halo_copy(s, hop, 1, 0).start()

    def hand_on(s):
        if s == steps - 1:
            @pl.when(jnp.logical_not(is_last))
            def _():
                hand_copy().start()

    for load in loads[:2]:
        load.wait()

    @pl.when(is_first)
    def _():
        for hop in range(hops):
            halo_out[0, hop, 0:members] = forcing[0, rows(tab[at.send + hop]), :].astype(BF16)
        send_listed(0)
        for c in range(cols):
            value = forcing[0, rows(c), :]
            traj[0, c] = value
            if steps > 1:
                xb[1, c, 0:members] = value.astype(BF16)

    @pl.when(jnp.logical_not(is_first))
    def _():
        jac_copy(0).wait()
        hand_copy().wait_recv()
        fix_copy().wait_recv()
        subset_sums([fix_in[hop] for hop in range(hops)])
        for c in range(cols):
            value = xin[c] + subset[tab[at.reads + c]]
            xin[c] = value
            xb[0, c, 0:members] = value.astype(BF16)
        advance(0, xin)

    for s in range(1, steps):
        jac_copy(s).wait()
        advance(s, traj.at[s - 1])

    for load in loads[2:]:
        load.wait()
    for s in range(steps):
        for c in range(cols):
            misfit[s, c] = error_weight[pl.ds(c, 1), :] * (traj[s, c] - observed[s, rows(c), :])
            traj_out[s, rows(c), :] = traj[s, c]

    def add_back(landing):
        subset_sums([back[landing, hop] for hop in range(hops)])

    def transpose_borders(s, value_of):
        for hop in range(hops):
            spot = blocks - hops + hop
            value = value_of(tab[at.column + spot]).astype(BF16)
            back_out[s, hop] = jnp.dot(
                value, jac[s][tab[at.perm + spot]], preferred_element_type=F32)
            if s > 0:
                back_copy(s, hop, 0, s - 1).start()
            else:
                back_copy(s, hop, -1, steps - 1).start()

    def keep_adjoint(s, value_of):
        for c in range(cols):
            value = value_of(c)
            adj[s, c] = value
            adj_b[c, 0:members] = value.astype(BF16)

    def own_part(s, c):
        return damping[pl.ds(c, 1), :] * adj[s, c] + sums[tab[at.last + c]]

    def transpose_step(s):
        blank = jnp.zeros((ROWS, lev), BF16)

        def some(g, total):
            for i in range(half):
                first = (g * half + i) * tiles
                turned = [adj_b[tab[at.column + first + n]] for n in range(tiles)]
                held = [jac[s][tab[at.perm + first + n]] for n in range(tiles)]
                if tiles == 4:
                    left = [jnp.concatenate([w, blank], axis=1) for w in turned[:2]]
                    left += [jnp.concatenate([blank, w], axis=1) for w in turned[2:]]
                    left = jnp.concatenate(left, axis=0)
                    upper = jnp.concatenate(held[:2], axis=1)
                    lower = jnp.concatenate(held[2:], axis=1)
                    right = jnp.concatenate([upper, lower], axis=0)
                else:
                    left, right = turned[0], held[0]
                spread = jnp.dot(left, right, preferred_element_type=F32)
                for n in range(tiles):
                    lane = n % 2 * lev
                    part = spread[n * ROWS : n * ROWS + members, lane : lane + lev]
                    total = part + scalar(at.keep + first + n) * total
                    sums[first + n] = total
            return total

        lax.fori_loop(0, blocks // tiles // half, some, jnp.zeros((members, lev), F32))

    top = steps - 1

    @pl.when(is_last)
    def _():
        def value_of(c):
            return misfit[top, c]

        if top > 0:
            transpose_borders(top, value_of)
        keep_adjoint(top, value_of)

    @pl.when(jnp.logical_not(is_last))
    def _():
        for hop in range(hops):
            back_copy(0, hop, 0, top).wait_recv()
        add_back(top)
        cin_copy().wait_recv()

        def value_of(c):
            return misfit[top, c] + cin[c] + subset[tab[at.listed + c]]

        if top > 0:
            transpose_borders(top, value_of)
        keep_adjoint(top, value_of)

    for s in range(top, 0, -1):
        transpose_step(s)
        for hop in range(hops):
            back_copy(0, hop, 0, s - 1).wait_recv()
        add_back(s - 1)

        def value_of(c, s=s):
            return misfit[s - 1, c] + own_part(s, c) + subset[tab[at.listed + c]]

        if s > 1:
            transpose_borders(s - 1, value_of)
        else:
            @pl.when(jnp.logical_not(is_first))
            def _():
                transpose_borders(0, value_of)

        keep_adjoint(s - 1, value_of)

    @pl.when(jnp.logical_not(is_first))
    def _():
        transpose_step(0)
        for c in range(cols):
            cout[c] = own_part(0, c)
        cin_copy().start()

    for s in range(steps):
        for c in range(cols):
            grad[s, rows(c), :] = forcing_weight[...] * forcing[s, rows(c), :] + adj[s, c]

    @pl.when(jnp.logical_not(is_first))
    def _():
        for hop in range(hops):
            back_copy(0, hop, -1, steps - 1).wait_send()
        cin_copy().wait_send()

    for s in range(1, steps):
        for hop in range(hops):
            back_copy(s, hop, 0, s - 1).wait_send()
            halo_copy(s - 1, hop, 0, s).wait_send()

    @pl.when(jnp.logical_not(is_last))
    def _():
        for hop in range(hops):
            halo_copy(steps - 1, hop, 1, 0).wait_send()
        hand_copy().wait_send()
        fix_copy().wait_send()


def copy_kernel(first_in, second_in, first_out, second_out, first, second, sem):
    loads = [
        pltpu.make_async_copy(first_in, first, sem.at[0]),
        pltpu.make_async_copy(second_in, second, sem.at[1]),
    ]
    stores = [
        pltpu.make_async_copy(first, first_out, sem.at[2]),
        pltpu.make_async_copy(second, second_out, sem.at[3]),
    ]
    for load in loads:
        load.start()
    for load, store in zip(loads, stores):
        load.wait()
        store.start()
    for store in stores:
        store.wait()


def on_device(
    sizes, forcing, observed, jacobian, block_index, send_list, damping, error_weight, forcing_weight
):
    steps, cols, members, lev = forcing.shape
    neigh = jacobian.shape[2]
    hops = send_list.shape[0]
    blocks = cols * neigh
    tab = index_tables(block_index, send_list)
    vmem = pl.BlockSpec(memory_space=pltpu.VMEM)
    far = pl.BlockSpec(memory_space=pl.ANY)
    flat = (steps, members * cols, lev)

    def by_member(array):
        return array.transpose(0, 2, 1, 3).reshape(flat)

    def by_column(array):
        return array.reshape(steps, members, cols, lev).transpose(0, 2, 1, 3)

    state = (cols, members, lev)
    dma = pltpu.SemaphoreType.DMA
    trajectory, gradient = pl.pallas_call(
        functools.partial(kernel, sizes),
        out_shape=(jax.ShapeDtypeStruct(flat, F32),) * 2,
        in_specs=[pl.BlockSpec(memory_space=pltpu.SMEM)] + [far] * 6,
        out_specs=(vmem, vmem),
        scratch_shapes=[
            pltpu.VMEM(flat, F32), pltpu.VMEM(flat, F32),
            pltpu.VMEM((cols, lev), F32), pltpu.VMEM((cols, lev), F32), pltpu.VMEM((1, lev), F32),
            dma((5,)),
            pltpu.VMEM(forcing.shape, F32),
            pltpu.VMEM(forcing.shape, F32),
            pltpu.VMEM((2 ** hops, members, lev), F32),
            pltpu.VMEM(state, F32),
            pltpu.VMEM((hops, members, lev), F32), pltpu.VMEM((hops, members, lev), F32),
            dma(()), dma(()),
            [pltpu.VMEM((blocks, lev, lev), BF16) for _ in range(steps)],
            pltpu.VMEM(state, F32),
            pltpu.VMEM((steps, cols + 1, ROWS, lev), BF16),
            pltpu.VMEM((steps, hops, ROWS, lev), BF16),
            pltpu.VMEM((steps, hops, ROWS, lev), BF16),
            pltpu.VMEM(forcing.shape, F32),
            pltpu.VMEM((cols, ROWS, lev), BF16),
            pltpu.VMEM((blocks + 1, members, lev), F32),
            pltpu.VMEM((steps, hops, members, lev), F32),
            pltpu.VMEM((steps, hops, members, lev), F32),
            pltpu.VMEM(state, F32),
            pltpu.VMEM(state, F32),
            dma((steps,)),
            dma((steps, hops)), dma((steps, hops)), dma(()), dma(()),
            dma((steps, hops)), dma((steps, hops)), dma(()), dma(()),
        ],
        compiler_params=pltpu.CompilerParams(
            collective_id=0, has_side_effects=True, vmem_limit_bytes=63 * 1024 * 1024),
    )(
        tab, by_member(forcing), by_member(observed), jacobian.reshape(steps, blocks, lev, lev),
        damping, error_weight, forcing_weight.reshape(1, lev),
    )
    trajectory, gradient = pl.pallas_call(
        copy_kernel,
        out_shape=(jax.ShapeDtypeStruct(flat, F32),) * 2,
        in_specs=[far, far],
        out_specs=(far, far),
        scratch_shapes=[pltpu.VMEM(flat, F32), pltpu.VMEM(flat, F32), dma((4,))],
        compiler_params=pltpu.CompilerParams(vmem_limit_bytes=63 * 1024 * 1024),
    )(trajectory, gradient)
    return by_column(trajectory), by_column(gradient)


def solution(mesh):
    sizes = (mesh.shape["space"], mesh.shape["tm"])
    in_specs = (
        P("tm", "space", None, None),
        P("tm", "space", None, None),
        P("tm", "space", None, None, None),
        P("space", None),
        P("space", None),
        P("space", None),
        P("space", None),
        P(),
    )
    out_specs = (P("tm", "space", None, None), P("tm", "space", None, None))
    return jax.shard_map(
        functools.partial(on_device, sizes), mesh=mesh, in_specs=in_specs, out_specs=out_specs,
        check_vma=False,
    )
```

```python
import functools
import jax
import jax.numpy as jnp
from jax import lax
from jax.experimental import pallas as pl
from jax.experimental.pallas import tpu as pltpu
from jax.sharding import PartitionSpec as P

OFFSETS = (1, -1, 2, -2)
ROWS = 32
MESH = pl.DeviceIdType.MESH
F32 = jnp.float32
BF16 = jnp.bfloat16


class Tables:
    def __init__(self, cols, neigh, hops):
        blocks = cols * neigh
        self.source = 0
        self.perm = self.source + blocks
        self.column = self.perm + blocks
        self.keep = self.column + blocks
        self.last = self.keep + blocks
        self.reads = self.last + cols
        self.listed = self.reads + cols
        self.send = self.listed + cols


def index_tables(block_index, send_list):
    cols, neigh = block_index.shape
    hops = send_list.shape[0]
    blocks = cols * neigh
    flat = block_index.reshape(-1)
    number = jnp.arange(blocks, dtype=jnp.int32)
    key = flat * blocks + number
    rank = jnp.sum((key[None, :] < key[:, None]).astype(jnp.int32), axis=1)
    chosen = rank[None, :] == number[:, None]
    perm = jnp.sum(jnp.where(chosen, number[None, :], 0), axis=1)
    ordered = jnp.sum(jnp.where(chosen, flat[None, :], 0), axis=1)
    keep = jnp.concatenate([jnp.zeros((1,), jnp.int32), (ordered[1:] == ordered[:-1]).astype(jnp.int32)])
    column = jnp.arange(cols, dtype=jnp.int32)
    upto = jnp.sum((flat[None, :] <= column[:, None]).astype(jnp.int32), axis=1)
    own = jnp.sum((flat[None, :] == column[:, None]).astype(jnp.int32), axis=1)
    last = jnp.where(own > 0, upto - 1, blocks)
    source = jnp.where(flat < cols, flat, cols)
    hop = jnp.arange(hops, dtype=jnp.int32)
    reads = jnp.any(block_index[:, :, None] == (cols + hop)[None, None, :], axis=1)
    reads = jnp.sum(jnp.where(reads, 1 << hop, 0), axis=1)
    listed = jnp.sum(jnp.where(send_list[:, 0][None, :] == column[:, None], 1 << hop, 0), axis=1)
    parts = [source, perm, perm // neigh, keep, last, reads, listed, send_list.reshape(-1)]
    return jnp.concatenate(parts)


def kernel(
    sizes,
    tab, forcing_hbm, observed_hbm, jac_hbm, damping_hbm, error_weight_hbm, forcing_weight_hbm,
    traj_out, grad,
    forcing, observed, damping, error_weight, forcing_weight, load_sem, traj, misfit, subset, part, fix_out, fix_in, fix_send, fix_recv, jac, xin, xb, halo, halo_out, adj, adj_b, sums, back, back_out, cin, cout,
    jac_sem, halo_send, halo_recv, hand_send, hand_recv,
    back_send, back_recv, cin_send, cin_recv,
):
    space, count = sizes
    steps, cols, members, lev = traj.shape
    neigh = jac[0].shape[0] // cols
    hops = halo.shape[1]
    blocks = cols * neigh
    at = Tables(cols, neigh, hops)
    me = lax.axis_index("space")
    turn = lax.axis_index("tm")
    is_first = turn == 0
    is_last = turn == count - 1
    pair = 2 if cols % 2 == 0 else 1
    group = cols // pair // 2 if cols // pair % 2 == 0 else cols // pair
    tiles = 4 if blocks % 4 == 0 else 1
    half = blocks // tiles // 2 if blocks // tiles % 2 == 0 else blocks // tiles

    def place(distance, later):
        return {"space": lax.rem(me + distance + 2 * space, space), "tm": turn + later}

    def jac_copy(s):
        return pltpu.make_async_copy(jac_hbm.at[s], jac[s], jac_sem.at[s])

    def halo_copy(s, hop, later, landing):
        return pltpu.make_async_remote_copy(
            src_ref=halo_out.at[s, hop], dst_ref=halo.at[landing, hop],
            send_sem=halo_send.at[s, hop], recv_sem=halo_recv.at[landing, hop],
            device_id=place(OFFSETS[hop], later), device_id_type=MESH)

    def hand_copy():
        return pltpu.make_async_remote_copy(
            src_ref=part, dst_ref=xin, send_sem=hand_send, recv_sem=hand_recv,
            device_id=place(0, 1), device_id_type=MESH)

    def fix_copy():
        return pltpu.make_async_remote_copy(
            src_ref=fix_out, dst_ref=fix_in, send_sem=fix_send, recv_sem=fix_recv,
            device_id=place(0, 1), device_id_type=MESH)

    def back_copy(s, hop, later, landing):
        return pltpu.make_async_remote_copy(
            src_ref=back_out.at[s, hop], dst_ref=back.at[landing, hop],
            send_sem=back_send.at[s, hop], recv_sem=back_recv.at[landing, hop],
            device_id=place(-OFFSETS[hop], later), device_id_type=MESH)

    def cin_copy():
        return pltpu.make_async_remote_copy(
            src_ref=cout, dst_ref=cin, send_sem=cin_send, recv_sem=cin_recv,
            device_id=place(0, -1), device_id_type=MESH)

    @pl.when(jnp.logical_not(is_first))
    def _():
        jac_copy(0).start()

    for s in range(1, steps):
        jac_copy(s).start()

    loads = [
        pltpu.make_async_copy(source, target, load_sem.at[i])
        for i, (source, target) in enumerate([
            (forcing_hbm, forcing), (damping_hbm, damping), (observed_hbm, observed),
            (error_weight_hbm, error_weight), (forcing_weight_hbm, forcing_weight)])
    ]
    for load in loads:
        load.start()

    def rows(c):
        return pl.ds(c, members, stride=cols)

    barrier = pltpu.get_barrier_semaphore()

    def greet(later):
        for distance in OFFSETS + ((0,) if later else ()):
            pl.semaphore_signal(barrier, inc=1, device_id=place(distance, later), device_id_type=MESH)

    greet(0)

    @pl.when(jnp.logical_not(is_first))
    def _():
        greet(-1)

    @pl.when(jnp.logical_not(is_last))
    def _():
        greet(1)

    for s in range(steps):
        xb[s, cols] = jnp.zeros((ROWS, lev), BF16)
    sums[blocks] = jnp.zeros((members, lev), F32)
    sides = jnp.where(is_first, 0, 1) + jnp.where(is_last, 0, 1)
    pl.semaphore_wait(barrier, hops + sides * (hops + 1))

    def scalar(index):
        return tab[index].astype(F32)

    def subset_sums(terms):
        held = [jnp.zeros((members, lev), F32)]
        for term in terms:
            held = held + [term if i == 0 else value + term for i, value in enumerate(held)]
        for i, value in enumerate(held):
            subset[i] = value

    def advance(s, before):
        def some(g, carry):
            for i in range(group):
                first = (g * group + i) * pair
                left, right = [], []
                for r in range(pair):
                    here = (first + r) * neigh
                    left.append(jnp.concatenate([xb[s, tab[at.source + here + k]] for k in range(neigh)], axis=1))
                    right.append(jnp.concatenate([jac[s][here + k] for k in range(neigh)], axis=1))
                mixed = lax.dot_general(
                    jnp.concatenate(left, axis=0), jnp.concatenate(right, axis=0),
                    (((1,), (1,)), ((), ())), preferred_element_type=F32)
                for r in range(pair):
                    c = first + r
                    damp = damping[pl.ds(c, 1), :]
                    own = mixed[r * ROWS : r * ROWS + members, r * lev : (r + 1) * lev]
                    part[c] = damp * before[c] + forcing[s, rows(c), :] + own
            return carry

        lax.fori_loop(0, cols // pair // group, some, 0)
        hand_on(s)
        remote = []
        for hop in range(hops):
            halo_copy(0, hop, 0, s).wait_recv()
        for hop in range(hops):
            block = tab[at.perm + blocks - hops + hop]
            remote.append(lax.dot_general(
                halo[s, hop], jac[s][block], (((1,), (1,)), ((), ())),
                preferred_element_type=F32)[:members])
        if s == steps - 1:
            for hop in range(hops):
                fix_out[hop] = remote[hop]

            @pl.when(jnp.logical_not(is_last))
            def _():
                fix_copy().start()

        subset_sums(remote)
        for hop in range(hops):
            c = tab[at.send + hop]
            value = part[c] + subset[tab[at.reads + c]]
            halo_out[s, hop, 0:members] = value.astype(BF16)
        send_listed(s)
        for c in range(cols):
            value = part[c] + subset[tab[at.reads + c]]
            traj[s, c] = value
            if s < steps - 1:
                xb[s + 1, c, 0:members] = value.astype(BF16)

    def send_listed(s):
        if s < steps - 1:
            for hop in range(hops):
                halo_copy(s, hop, 0, s + 1).start()
        else:
            @pl.when(jnp.logical_not(is_last))
            def _():
                for hop in range(hops):
                    halo_copy(s, hop, 1, 0).start()

    def hand_on(s):
        if s == steps - 1:
            @pl.when(jnp.logical_not(is_last))
            def _():
                hand_copy().start()

    for load in loads[:2]:
        load.wait()

    @pl.when(is_first)
    def _():
        for hop in range(hops):
            halo_out[0, hop, 0:members] = forcing[0, rows(tab[at.send + hop]), :].astype(BF16)
        send_listed(0)
        for c in range(cols):
            value = forcing[0, rows(c), :]
            traj[0, c] = value
            if steps > 1:
                xb[1, c, 0:members] = value.astype(BF16)

    @pl.when(jnp.logical_not(is_first))
    def _():
        jac_copy(0).wait()
        hand_copy().wait_recv()
        fix_copy().wait_recv()
        subset_sums([fix_in[hop] for hop in range(hops)])
        for c in range(cols):
            value = xin[c] + subset[tab[at.reads + c]]
            xin[c] = value
            xb[0, c, 0:members] = value.astype(BF16)
        advance(0, xin)

    for s in range(1, steps):
        jac_copy(s).wait()
        advance(s, traj.at[s - 1])

    for load in loads[2:]:
        load.wait()
    for s in range(steps):
        for c in range(cols):
            misfit[s, c] = error_weight[pl.ds(c, 1), :] * (traj[s, c] - observed[s, rows(c), :])
            traj_out[s, rows(c), :] = traj[s, c]

    def add_back(landing):
        subset_sums([back[landing, hop] for hop in range(hops)])

    def transpose_borders(s, value_of):
        for hop in range(hops):
            spot = blocks - hops + hop
            value = value_of(tab[at.column + spot]).astype(BF16)
            back_out[s, hop] = jnp.dot(
                value, jac[s][tab[at.perm + spot]], preferred_element_type=F32)
            if s > 0:
                back_copy(s, hop, 0, s - 1).start()
            else:
                back_copy(s, hop, -1, steps - 1).start()

    def keep_adjoint(s, value_of):
        for c in range(cols):
            value = value_of(c)
            adj[s, c] = value
            adj_b[c, 0:members] = value.astype(BF16)

    def own_part(s, c):
        return damping[pl.ds(c, 1), :] * adj[s, c] + sums[tab[at.last + c]]

    def transpose_step(s):
        blank = jnp.zeros((ROWS, lev), BF16)

        def some(g, total):
            for i in range(half):
                first = (g * half + i) * tiles
                turned = [adj_b[tab[at.column + first + n]] for n in range(tiles)]
                held = [jac[s][tab[at.perm + first + n]] for n in range(tiles)]
                if tiles == 4:
                    left = [jnp.concatenate([w, blank], axis=1) for w in turned[:2]]
                    left += [jnp.concatenate([blank, w], axis=1) for w in turned[2:]]
                    left = jnp.concatenate(left, axis=0)
                    upper = jnp.concatenate(held[:2], axis=1)
                    lower = jnp.concatenate(held[2:], axis=1)
                    right = jnp.concatenate([upper, lower], axis=0)
                else:
                    left, right = turned[0], held[0]
                spread = jnp.dot(left, right, preferred_element_type=F32)
                for n in range(tiles):
                    lane = n % 2 * lev
                    part = spread[n * ROWS : n * ROWS + members, lane : lane + lev]
                    total = part + scalar(at.keep + first + n) * total
                    sums[first + n] = total
            return total

        lax.fori_loop(0, blocks // tiles // half, some, jnp.zeros((members, lev), F32))

    top = steps - 1

    @pl.when(is_last)
    def _():
        def value_of(c):
            return misfit[top, c]

        if top > 0:
            transpose_borders(top, value_of)
        keep_adjoint(top, value_of)

    @pl.when(jnp.logical_not(is_last))
    def _():
        for hop in range(hops):
            back_copy(0, hop, 0, top).wait_recv()
        add_back(top)
        cin_copy().wait_recv()

        def value_of(c):
            return misfit[top, c] + cin[c] + subset[tab[at.listed + c]]

        if top > 0:
            transpose_borders(top, value_of)
        keep_adjoint(top, value_of)

    for s in range(top, 0, -1):
        transpose_step(s)
        for hop in range(hops):
            back_copy(0, hop, 0, s - 1).wait_recv()
        add_back(s - 1)

        def value_of(c, s=s):
            return misfit[s - 1, c] + own_part(s, c) + subset[tab[at.listed + c]]

        if s > 1:
            transpose_borders(s - 1, value_of)
        else:
            @pl.when(jnp.logical_not(is_first))
            def _():
                transpose_borders(0, value_of)

        keep_adjoint(s - 1, value_of)

    @pl.when(jnp.logical_not(is_first))
    def _():
        transpose_step(0)
        for c in range(cols):
            cout[c] = own_part(0, c)
        cin_copy().start()

    for s in range(steps):
        for c in range(cols):
            grad[s, rows(c), :] = forcing_weight[...] * forcing[s, rows(c), :] + adj[s, c]

    @pl.when(jnp.logical_not(is_first))
    def _():
        for hop in range(hops):
            back_copy(0, hop, -1, steps - 1).wait_send()
        cin_copy().wait_send()

    for s in range(1, steps):
        for hop in range(hops):
            back_copy(s, hop, 0, s - 1).wait_send()
            halo_copy(s - 1, hop, 0, s).wait_send()

    @pl.when(jnp.logical_not(is_last))
    def _():
        for hop in range(hops):
            halo_copy(steps - 1, hop, 1, 0).wait_send()
        hand_copy().wait_send()
        fix_copy().wait_send()


def copy_kernel(first_in, second_in, first_out, second_out, first, second, sem):
    loads = [
        pltpu.make_async_copy(first_in, first, sem.at[0]),
        pltpu.make_async_copy(second_in, second, sem.at[1]),
    ]
    stores = [
        pltpu.make_async_copy(first, first_out, sem.at[2]),
        pltpu.make_async_copy(second, second_out, sem.at[3]),
    ]
    for load in loads:
        load.start()
    for load, store in zip(loads, stores):
        load.wait()
        store.start()
    for store in stores:
        store.wait()


def on_device(
    sizes, forcing, observed, jacobian, block_index, send_list, damping, error_weight, forcing_weight
):
    steps, cols, members, lev = forcing.shape
    neigh = jacobian.shape[2]
    hops = send_list.shape[0]
    blocks = cols * neigh
    tab = index_tables(block_index, send_list)
    vmem = pl.BlockSpec(memory_space=pltpu.VMEM)
    far = pl.BlockSpec(memory_space=pl.ANY)
    flat = (steps, members * cols, lev)

    def by_member(array):
        return array.transpose(0, 2, 1, 3).reshape(flat)

    def by_column(array):
        return array.reshape(steps, members, cols, lev).transpose(0, 2, 1, 3)

    state = (cols, members, lev)
    dma = pltpu.SemaphoreType.DMA
    trajectory, gradient = pl.pallas_call(
        functools.partial(kernel, sizes),
        out_shape=(jax.ShapeDtypeStruct(flat, F32),) * 2,
        in_specs=[pl.BlockSpec(memory_space=pltpu.SMEM)] + [far] * 6,
        out_specs=(vmem, vmem),
        scratch_shapes=[
            pltpu.VMEM(flat, F32), pltpu.VMEM(flat, F32),
            pltpu.VMEM((cols, lev), F32), pltpu.VMEM((cols, lev), F32), pltpu.VMEM((1, lev), F32),
            dma((5,)),
            pltpu.VMEM(forcing.shape, F32),
            pltpu.VMEM(forcing.shape, F32),
            pltpu.VMEM((2 ** hops, members, lev), F32),
            pltpu.VMEM(state, F32),
            pltpu.VMEM((hops, members, lev), F32), pltpu.VMEM((hops, members, lev), F32),
            dma(()), dma(()),
            [pltpu.VMEM((blocks, lev, lev), BF16) for _ in range(steps)],
            pltpu.VMEM(state, F32),
            pltpu.VMEM((steps, cols + 1, ROWS, lev), BF16),
            pltpu.VMEM((steps, hops, ROWS, lev), BF16),
            pltpu.VMEM((steps, hops, ROWS, lev), BF16),
            pltpu.VMEM(forcing.shape, F32),
            pltpu.VMEM((cols, ROWS, lev), BF16),
            pltpu.VMEM((blocks + 1, members, lev), F32),
            pltpu.VMEM((steps, hops, members, lev), F32),
            pltpu.VMEM((steps, hops, members, lev), F32),
            pltpu.VMEM(state, F32),
            pltpu.VMEM(state, F32),
            dma((steps,)),
            dma((steps, hops)), dma((steps, hops)), dma(()), dma(()),
            dma((steps, hops)), dma((steps, hops)), dma(()), dma(()),
        ],
        compiler_params=pltpu.CompilerParams(
            collective_id=0, has_side_effects=True, vmem_limit_bytes=63 * 1024 * 1024),
    )(
        tab, by_member(forcing), by_member(observed), jacobian.reshape(steps, blocks, lev, lev),
        damping, error_weight, forcing_weight.reshape(1, lev),
    )
    trajectory, gradient = pl.pallas_call(
        copy_kernel,
        out_shape=(jax.ShapeDtypeStruct(flat, F32),) * 2,
        in_specs=[far, far],
        out_specs=(far, far),
        scratch_shapes=[pltpu.VMEM(flat, F32), pltpu.VMEM(flat, F32), dma((4,))],
        compiler_params=pltpu.CompilerParams(vmem_limit_bytes=63 * 1024 * 1024),
    )(trajectory, gradient)
    return by_column(trajectory), by_column(gradient)


def solution(mesh):
    sizes = (mesh.shape["space"], mesh.shape["tm"])
    in_specs = (
        P("tm", "space", None, None),
        P("tm", "space", None, None),
        P("tm", "space", None, None, None),
        P("space", None),
        P("space", None),
        P("space", None),
        P("space", None),
        P(),
    )
    out_specs = (P("tm", "space", None, None), P("tm", "space", None, None))
    return jax.shard_map(
        functools.partial(on_device, sizes), mesh=mesh, in_specs=in_specs, out_specs=out_specs,
        check_vma=False,
    )
```
